256 devices in a mesh: row: 16 (over z, core), col: 4 (over x), rep: 4 (over y).
Axes of the slice: x: 4, y: 4, z: 8, core: 2. Of those that a mesh axis runs over, the one named last changes fastest.
Arguments:
- front: float32 [4096, 256, 256], P(('row', 'col', 'rep')), may hold values from -6 to 6
- pivots: bfloat16 [4, 2, 256, 256], P('rep'), may hold values from -0.375 to 0.375
- upper_link: bfloat16 [4, 256, 256], P('rep'), may hold values from -0.375 to 0.375
- lower_link: bfloat16 [4, 256, 256], P('rep'), may hold values from -0.375 to 0.375
- lower_panels: bfloat16 [4, 2, 32, 256, 256], P('rep', None, 'row', 'col'), may hold values from -6 to 6
- upper_panels: bfloat16 [4, 2, 96, 256, 256], P('rep', None, 'col', 'row'), may hold values from -0.375 to 0.375
- lower_slots: int32 [4, 2, 32], P(None, None, 'row'), may hold values from -1 to 1, as said below
- upper_slots: int32 [4, 2, 96], P(None, None, 'col'), may hold values from -1 to 31, as said below
- owner_map: int32 [64, 64], P(('row', 'col')), may hold values from 0 to 63, each once within a row
Outputs:
- schur: float32 [4096, 256, 256], P(('row', 'col', 'rep'))
The draws below stay inside these ranges and needn't reach their ends.
Inputs may be any that keep to these rules, and one draw needn't show every extreme that they name: `lower_slots`: for each replica, panel and process row r, the 2 entries from r * 2 on name distinct local block rows, filled entries first and -1 for the empty rest; half of them or more are filled, and in every replica and panel some process row has all filled. `upper_slots`: for each replica, panel and process column c, the 24 entries from c * 24 on name distinct local block columns, filled entries first and -1 for the empty rest; half of them or more are filled, and in every replica and panel some process column has all filled. `owner_map`: row t is a permutation of the local block indices e = a * 32 + b of the tile of process row t // 4 and process column t % 4; entries q * 16 to (q + 1) * 16 - 1 are the blocks whose result replica q holds.
All inputs are finite; a program needn't handle non-finite values.
Results may differ from the reference program's by a relative error of at most 0.0095.
Values may be sent and summed in bfloat16 or wider, within the bound.
A program may use at most 192 MiB of HBM per device.

```python
import jax
import jax.numpy as jnp

B = 256
RB_DEV = 2
CB_DEV = 32
CS = 24
NAR = 32
NAC = 128
TILE = 64
NBLK = 4096
N_ROW = 16
N_COL = 4
N_REP = 4


def slot_lists(key, groups, capacity, choices_count):

    def draw_group(subkey):
        key_order, key_count, key_full = jax.random.split(subkey, 3)
        group_keys = jax.random.split(key_order, groups)
        orders = jax.vmap(lambda group_key: jax.random.permutation(group_key, choices_count)[:capacity])(group_keys)
        counts = jax.random.randint(key_count, (groups,), (capacity + 1) // 2, capacity + 1)
        full_row = jax.random.randint(key_full, (), 0, groups)
        counts = jnp.where(jnp.arange(groups) == full_row, capacity, counts)
        filled = jnp.arange(capacity)[None, :] < counts[:, None]
        return jnp.where(filled, orders, -1).reshape(groups * capacity).astype(jnp.int32)
    subkeys = jax.random.split(key, N_REP * 2)
    return jax.vmap(draw_group)(subkeys).reshape(N_REP, 2, groups * capacity)


def draw_lower_slots(key, part):
    key = jax.random.fold_in(key, 11)
    return slot_lists(key, N_ROW, RB_DEV, RB_DEV)


def draw_upper_slots(key, part):
    key = jax.random.fold_in(key, 12)
    return slot_lists(key, N_COL, CS, CB_DEV)


def steps_of(own_key, dims, cuts, low, largest):
    factor_of, own = 1.0, jax.random.fold_in(own_key, 6)
    for axis_at, blocks in cuts:
        draws = jnp.exp(jax.random.uniform(jax.random.fold_in(own, axis_at), (blocks,), jnp.float32, low / len(cuts), largest / len(cuts)))
        factor_of = factor_of * jnp.repeat(draws, dims[axis_at] // blocks).reshape([-1 if axis == axis_at else 1 for axis in range(len(dims))])
    return factor_of


def centred(own_key, dims, deviation, limit, cuts=(), held_as=jnp.bfloat16):
    loudness = steps_of(own_key, dims, cuts, -0.22, 0.18) if cuts else 1.0
    entries = jax.random.normal(own_key, dims, jnp.float32) * deviation * loudness
    return jnp.minimum(jnp.maximum(entries, -limit), limit).astype(held_as)


def setup_inputs(seed: int = 0) -> dict:
    seeds = jax.random.split(jax.random.key(seed), 10)
    return {
        "front": centred(seeds[0], (NBLK, B, B), 1.0, 6.0, ((0, 256),), jnp.float32),
        "pivots": centred(seeds[1], (N_REP, 2, B, B), B ** -0.5, 0.375, ((0, 4),)),
        "upper_link": centred(seeds[2], (N_REP, B, B), B ** -0.5, 0.375, ((0, 4),)),
        "lower_link": centred(seeds[3], (N_REP, B, B), B ** -0.5, 0.375, ((0, 4),)),
        "lower_panels": centred(seeds[4], (N_REP, 2, N_ROW * RB_DEV, B, B), 1.0, 6.0, ((0, 4), (2, 16), (3, 4))),
        "upper_panels": centred(seeds[5], (N_REP, 2, N_COL * CS, B, B), B ** -0.5, 0.375, ((0, 4), (2, 4), (3, 16))),
        "lower_slots": draw_lower_slots(jax.random.fold_in(seeds[9], 71), 0),
        "upper_slots": draw_upper_slots(jax.random.fold_in(seeds[9], 71), 0),
        "owner_map": jax.vmap(lambda own: jax.random.permutation(own, TILE))(jax.random.split(seeds[8], (N_ROW * N_COL))).reshape((N_ROW * N_COL, TILE)).astype(jnp.int32),
    }


def place_blocks(blocks, places, last_row):
    zeroed = jnp.zeros((last_row + 1,) + blocks.shape[1:], blocks.dtype)
    filled = zeroed.at[places].set(blocks)
    return filled.at[last_row].set(jnp.zeros(blocks.shape[1:], blocks.dtype))


def front_rows(slot_values, group_size, stride, last_row):
    position = jnp.arange(slot_values.shape[-1], dtype=jnp.int32)
    group_ids = position // group_size
    return jnp.where(slot_values >= 0, slot_values * stride + group_ids, last_row).astype(jnp.int32)


def reference(front, pivots, upper_link, lower_link, lower_panels, upper_panels, lower_slots, upper_slots, owner_map):
    accumulated = jnp.zeros((NAR * B, NAC * B), jnp.float32)
    for replica in range(N_REP):
        row_ids = front_rows(lower_slots[replica], RB_DEV, N_ROW, NAR)
        col_ids = front_rows(upper_slots[replica], CS, N_COL, NAC)
        first_pivot = pivots[replica, 0].astype(jnp.float32)
        second_pivot = pivots[replica, 1].astype(jnp.float32)
        lower_first = jnp.einsum("sxy,yz->sxz", lower_panels[replica, 0].astype(jnp.float32), first_pivot).astype(jnp.bfloat16)
        first_dense = place_blocks(lower_first, row_ids[0], NAR)
        lower_carried = first_dense[row_ids[1]]
        carried_term = jnp.einsum("sxy,yz->sxz", lower_carried.astype(jnp.float32), upper_link[replica].astype(jnp.float32))
        lower_diff = (lower_panels[replica, 1].astype(jnp.float32) - carried_term).astype(jnp.bfloat16)
        lower_second = jnp.einsum("sxy,yz->sxz", lower_diff.astype(jnp.float32), second_pivot).astype(jnp.bfloat16)
        second_dense = place_blocks(lower_second, row_ids[1], NAR)
        link_row = jnp.dot(lower_link[replica], pivots[replica, 0], preferred_element_type=jnp.float32).astype(jnp.bfloat16)
        upper_first = upper_panels[replica, 0]
        upper_first_dense = place_blocks(upper_first, col_ids[0], NAC)
        upper_carried = upper_first_dense[col_ids[1]]
        shifted = jnp.einsum("xy,tyz->txz", link_row.astype(jnp.float32), upper_carried.astype(jnp.float32))
        upper_second = (upper_panels[replica, 1].astype(jnp.float32) - shifted).astype(jnp.bfloat16)
        upper_second_dense = place_blocks(upper_second, col_ids[1], NAC)
        lower_matrix = jnp.stack([first_dense[:NAR], second_dense[:NAR]]).transpose(1, 2, 0, 3).reshape(NAR * B, 2 * B)
        upper_matrix = jnp.stack([upper_first_dense[:NAC], upper_second_dense[:NAC]]).transpose(0, 2, 1, 3).reshape(2 * B, NAC * B)
        update = jnp.dot(lower_matrix, upper_matrix, preferred_element_type=jnp.float32).astype(jnp.bfloat16)
        accumulated = accumulated + update.astype(jnp.float32)
    positions = jnp.arange(NBLK, dtype=jnp.int32)
    tile_index = positions // TILE
    local_ids = owner_map[tile_index, positions % TILE]
    block_row = (local_ids // CB_DEV) * N_ROW + tile_index // N_COL
    block_col = (local_ids % CB_DEV) * N_COL + tile_index % N_COL
    blocks = accumulated.reshape(NAR, B, NAC, B)[block_row, :, block_col, :]
    return front - blocks
```

```python
import functools

import jax
import jax.numpy as jnp
from jax import lax
from jax.experimental import pallas as pl
from jax.experimental.pallas import tpu as pltpu
from jax.sharding import PartitionSpec as P

MESH = pl.DeviceIdType.MESH
NT = (((1,), (1,)), ((), ()))
B = 256
CH = 2
W = 32
SLOTS = 24
GROUPS = 6
SUBS = (0, 1, 3, 2)
LAST = ((0, 1), (2, 3))
ZN = 8


def main_kernel(
    inv_ref,
    lsl_ref,
    own_ref,
    u_ref,
    lp_ref,
    piv_ref,
    ul_ref,
    ll_ref,
    out_ref,
    pk,
    ug,
    ut,
    lb,
    lsel,
    lhs,
    acb,
    ctb,
    snd,
    a2a_s,
    a2a_r,
    ring_s,
    ring_r,
    sib_s,
    sib_r,
    ly_s,
    ly_r,
    lx_s,
    lx_r,
    shp_s,
    shp_r,
    loc_s,
):
    row = lax.axis_index("row")
    x = lax.axis_index("col")
    y = lax.axis_index("rep")
    z = row // 2
    core = row % 2

    def ydev(d):
        return (row, x, (y + d) % 4)

    def xdev(d):
        return (row, (x + d) % 4, y)

    def zdev(d):
        return (((z + d + ZN) % ZN) * 2 + core, x, y)

    sib = (z * 2 + 1 - core, x, y)

    def src_of(d):
        return ((z + d + ZN) % ZN) * 2 + core

    def rep_of(sub):
        return (y - SUBS[sub] + 4) % 4

    bar = pltpu.get_barrier_semaphore()
    partners = [ydev(1), ydev(2), ydev(3), xdev(1), xdev(2), xdev(3), zdev(1), zdev(-1), sib]
    for p in partners:
        pl.semaphore_signal(bar, inc=1, device_id=p, device_id_type=MESH)

    def pack(ch):
        parts = [
            u_ref[:, :, j, :, 128 * ch : 128 * ch + 128].reshape(2 * GROUPS * 16, 128)
            for j in range(4)
        ]
        for yy in range(4):
            piece = jnp.concatenate([p[:, W * yy : W * yy + W] for p in parts], axis=1)
            pk[ch, yy] = piece.reshape(2, GROUPS, 16, 128)

    def remote(src, dst, ss, rs, dev):
        return pltpu.make_async_remote_copy(
            src_ref=src, dst_ref=dst, send_sem=ss, recv_sem=rs, device_id=dev, device_id_type=MESH
        )

    def a2a(ch, sub, receive=False):
        d = SUBS[sub]
        if receive:
            ref = ug.at[ch, row, rep_of(sub)]
            return remote(ref, ref, a2a_s.at[ch, sub - 1], a2a_r.at[ch, sub - 1], ydev(d))
        return remote(
            pk.at[ch, (y + d) % 4],
            ug.at[ch, row, y],
            a2a_s.at[ch, sub - 1],
            a2a_r.at[ch, sub - 1],
            ydev(d),
        )

    def ring(ch, way, step, sub, receive=False):
        sign = 1 if way == 0 else -1
        origin = src_of(-sign * (step + 1 if receive else step))
        ref = ug.at[ch, origin, rep_of(sub)]
        return remote(
            ref, ref, ring_s.at[ch, way, step, sub], ring_r.at[ch, way, step, sub], zdev(sign)
        )

    def sibling(ch, d, receive=False):
        s = (z + d + ZN) % ZN
        ref = ug.at[ch, s * 2 + (1 - core if receive else core)]
        return remote(ref, ref, sib_s.at[ch, d % ZN], sib_r.at[ch, d % ZN], sib)

    def ring_subs(way, step):
        return range(4) if step < 3 else LAST[way]

    def ring_first(ch, subs):
        for sub in subs:
            if sub:
                a2a(ch, sub, True).wait_recv()
            for way in range(2):
                ring(ch, way, 0, sub).start()

    def ring_step(ch, step):
        for sub in range(4):
            for way in range(2):
                if sub in ring_subs(way, step - 1):
                    ring(ch, way, step - 1, sub, True).wait_recv()
                    if step < 4 and sub in ring_subs(way, step):
                        ring(ch, way, step, sub).start()
        if step < 4:
            sibling(ch, -step).start()
            sibling(ch, step).start()
        else:
            sibling(ch, 4).start()

    def ly(sub, receive=False):
        d = SUBS[sub]
        ref = lb.at[rep_of(sub) if receive else y, x, pl.ds(0, 5)]
        return remote(ref, ref, ly_s.at[sub - 1], ly_r.at[sub - 1], ydev(d))

    def lx(sub, d, receive=False):
        ref = lb.at[rep_of(sub), (x - d + 4) % 4 if receive else x, pl.ds(0, 5)]
        return remote(ref, ref, lx_s.at[sub, d - 1], lx_r.at[sub, d - 1], xdev(d))

    def ship(ch, d, receive=False):
        if receive:
            ref = out_ref.at[ch, (y - d + 4) % 4]
            return remote(ref, ref, shp_s.at[ch, d - 1], shp_r.at[ch, d - 1], ydev(d))
        return remote(
            snd.at[ch, (y + d) % 4],
            out_ref.at[ch, y],
            shp_s.at[ch, d - 1],
            shp_r.at[ch, d - 1],
            ydev(d),
        )

    def lower_prep():
        first = jnp.dot(
            lp_ref[0].reshape(128, B), piv_ref[0], preferred_element_type=jnp.float32
        ).astype(jnp.bfloat16)
        lb[y, x, 0:2] = first.reshape(2, 64, B)
        wide = first.astype(jnp.float32)
        pieces = []
        for g in range(2):
            sg = lsl_ref[y * 2 + 1, g]
            hit0 = jnp.where((sg >= 0) & (sg == lsl_ref[y * 2, 0]), 1.0, 0.0)
            hit1 = jnp.where((sg >= 0) & (sg == lsl_ref[y * 2, 1]), 1.0, 0.0)
            pieces.append(wide[:64] * hit0 + wide[64:] * hit1)
        carried = jnp.concatenate(pieces, axis=0).astype(jnp.bfloat16)
        term = jnp.dot(carried, ul_ref[...], preferred_element_type=jnp.float32)
        diff = (lp_ref[1].reshape(128, B).astype(jnp.float32) - term).astype(jnp.bfloat16)
        second = jnp.dot(diff, piv_ref[1], preferred_element_type=jnp.float32).astype(jnp.bfloat16)
        lb[y, x, 2:4] = second.reshape(2, 64, B)
        link = jnp.dot(
            ll_ref[pl.ds(pl.multiple_of(x * 64, 64), 64), :],
            piv_ref[0],
            preferred_element_type=jnp.float32,
        ).astype(jnp.bfloat16)
        lb[y, x, 4] = link
        for q in range(4):
            for xx in range(4):
                lb[q, xx, 5] = jnp.zeros((64, B), jnp.bfloat16)

    def lower_select():
        for q in range(4):
            for k in range(2):
                s0 = lsl_ref[q * 2 + k, 0]
                s1 = lsl_ref[q * 2 + k, 1]
                for a in range(2):
                    at = jnp.where(s0 == a, 2 * k, jnp.where(s1 == a, 2 * k + 1, 5))
                    for xx in range(4):
                        lsel[
                            a * B + xx * 64 : a * B + xx * 64 + 64,
                            (2 * q + k) * B : (2 * q + k + 1) * B,
                        ] = lb[q, xx, at]

    def turn(ch):
        def step(i, carry):
            q, k = i // 2, i % 2
            for g in range(GROUPS):
                block = ug[ch, :, q, k, g].reshape(B, 128)
                ut[q, k, 4 * g : 4 * g + 4] = block.T.reshape(4, W, B)
            return carry

        lax.fori_loop(0, 8, step, 0)

    def arrange():
        def step(b, carry):
            for q in range(4):
                at0 = inv_ref[q * 3, b]
                at1 = inv_ref[q * 3 + 1, b]
                atc = inv_ref[q * 3 + 2, b]
                rows = pl.ds(pl.multiple_of(b * W, W), W)
                lhs[rows, 2 * q * B : 2 * q * B + B] = ut[q, 0, at0]
                lhs[rows, (2 * q + 1) * B : (2 * q + 2) * B] = ut[q, 1, at1]
                acb[q, rows, :] = ut[q, 0, atc]
            return carry

        lax.fori_loop(0, 32, step, 0)

    def second_upper():
        for q in range(4):
            link = lb[q, :, 4].reshape(B, B)

            def step(i, carry):
                rows = pl.ds(pl.multiple_of(i * 256, 256), 256)
                shift = lax.dot_general(
                    acb[q, rows, :], link, NT, preferred_element_type=jnp.float32
                )
                cols = slice((2 * q + 1) * B, (2 * q + 2) * B)
                lhs[rows, cols] = (lhs[rows, cols].astype(jnp.float32) - shift).astype(jnp.bfloat16)
                return carry

            lax.fori_loop(0, 4, step, 0)

    def multiply():
        def step(i, carry):
            rows = pl.ds(pl.multiple_of(i * 256, 256), 256)
            prod = lax.dot_general(
                lhs[rows, :], lsel[...], NT, preferred_element_type=jnp.float32
            ).astype(jnp.bfloat16)
            for a in range(2):
                ctb[a, pl.ds(i * 8, 8)] = prod[:, a * B : a * B + B].reshape(8, W, B)
            return carry

        lax.fori_loop(0, 4, step, 0)

    def choose(ch):
        def step(m, carry):
            e = own_ref[0, m]
            snd[ch, m // 16, m % 16] = ctb[e // 32, e % 32]
            return carry

        lax.fori_loop(0, 64, step, 0)

    def local_out(ch):
        return pltpu.make_async_copy(snd.at[ch, y], out_ref.at[ch, y], loc_s.at[ch])

    def start_ship(ch):
        for d in (1, 3, 2):
            ship(ch, d).start()
        local_out(ch).start()

    def wait_sibling(ch):
        for d in range(ZN):
            sibling(ch, d if d < 5 else d - ZN, True).wait_recv()

    for q in range(4):
        for k in range(2):
            ut[q, k, SLOTS] = jnp.zeros((W, B), jnp.bfloat16)
    pack(0)
    ug[0, row, y] = pk[0, y]
    pl.semaphore_wait(bar, len(partners))
    for sub in (1, 2, 3):
        a2a(0, sub).start()
    ring_first(0, (0,))
    lower_prep()
    for sub in (1, 2, 3):
        ly(sub).start()
    for d in (1, 3, 2):
        lx(0, d).start()
    pack(1)
    ug[1, row, y] = pk[1, y]
    for sub in (1, 2, 3):
        a2a(1, sub).start()
    ring_first(0, (1, 2, 3))
    sibling(0, 0).start()
    for sub in (1, 2, 3):
        ly(sub, True).wait_recv()
        for d in (1, 3, 2):
            lx(sub, d).start()
    ring_step(0, 1)
    ring_step(0, 2)
    ring_step(0, 3)
    ring_first(1, (0, 1, 2, 3))
    sibling(1, 0).start()
    for sub in range(4):
        for d in (1, 3, 2):
            lx(sub, d, True).wait_recv()
    lower_select()
    ring_step(0, 4)
    ring_step(1, 1)
    wait_sibling(0)
    turn(0)
    arrange()
    second_upper()
    ring_step(1, 2)
    multiply()
    choose(0)
    start_ship(0)
    ring_step(1, 3)
    ring_step(1, 4)
    wait_sibling(1)
    turn(1)
    arrange()
    second_upper()
    multiply()
    choose(1)
    start_ship(1)

    for ch in range(CH):
        for sub in (1, 2, 3):
            a2a(ch, sub).wait_send()
        for way in range(2):
            for st in range(4):
                for sub in ring_subs(way, st):
                    ring(ch, way, st, sub).wait_send()
        for d in range(ZN):
            sibling(ch, d if d < 5 else d - ZN).wait_send()
    for sub in range(4):
        if sub:
            ly(sub).wait_send()
        for d in (1, 2, 3):
            lx(sub, d).wait_send()
    for ch in range(CH):
        local_out(ch).wait()
        for d in (1, 2, 3):
            ship(ch, d).wait_send()
            ship(ch, d, True).wait_recv()


def finish_kernel(front_ref, got_ref, out_ref):
    for i in range(front_ref.shape[0]):
        block = got_ref[:, :, i].reshape(B, B)
        out_ref[i] = front_ref[i] - block.T.astype(jnp.float32)


def body(
    front,
    pivots,
    upper_link,
    lower_link,
    lower_panels,
    upper_panels,
    lower_slots,
    upper_slots,
    owner_map,
):
    names = jnp.arange(32, dtype=jnp.int32)
    same = upper_slots[:, :, None, :] == names[None, None, :, None]
    at = jnp.arange(SLOTS, dtype=jnp.int32)
    inv = jnp.min(jnp.where(same, at[None, None, None, :], SLOTS), axis=-1)
    carried = jnp.where(inv[:, 1] < SLOTS, inv[:, 0], SLOTS)
    inv = jnp.concatenate([inv, carried[:, None]], axis=1).reshape(12, 32)
    vmem = pl.BlockSpec(memory_space=pltpu.VMEM)
    smem = pl.BlockSpec(memory_space=pltpu.SMEM)
    dma = pltpu.SemaphoreType.DMA
    bf = jnp.bfloat16
    got = pl.pallas_call(
        main_kernel,
        out_shape=jax.ShapeDtypeStruct((CH, 4, 16, W, B), bf),
        in_specs=[smem] * 3 + [vmem] * 5,
        out_specs=pl.BlockSpec(memory_space=pl.ANY),
        scratch_shapes=[
            pltpu.VMEM((CH, 4, 2, GROUPS, 16, 128), bf),
            pltpu.VMEM((CH, 16, 4, 2, GROUPS, 16, 128), bf),
            pltpu.VMEM((4, 2, SLOTS + 1, W, B), bf),
            pltpu.VMEM((4, 4, 6, 64, B), bf),
            pltpu.VMEM((2 * B, 8 * B), bf),
            pltpu.VMEM((32 * W, 8 * B), bf),
            pltpu.VMEM((4, 32 * W, B), bf),
            pltpu.VMEM((2, 32, W, B), bf),
            pltpu.VMEM((CH, 4, 16, W, B), bf),
            dma((CH, 3)),
            dma((CH, 3)),
            dma((CH, 2, 4, 4)),
            dma((CH, 2, 4, 4)),
            dma((CH, ZN)),
            dma((CH, ZN)),
            dma((3,)),
            dma((3,)),
            dma((4, 3)),
            dma((4, 3)),
            dma((CH, 3)),
            dma((CH, 3)),
            dma((CH,)),
        ],
        compiler_params=pltpu.CompilerParams(
            collective_id=0, has_side_effects=True, vmem_limit_bytes=48 << 20
        ),
    )(
        inv,
        lower_slots.reshape(8, 2),
        owner_map,
        upper_panels[0].reshape(2, GROUPS, 4, 16, B),
        lower_panels[0],
        pivots[0],
        upper_link[0],
        lower_link[0],
    )
    return pl.pallas_call(
        finish_kernel,
        grid=(8,),
        out_shape=jax.ShapeDtypeStruct(front.shape, front.dtype),
        in_specs=[
            pl.BlockSpec((2, B, B), lambda i: (i, 0, 0)),
            pl.BlockSpec((CH, 4, 2, W, B), lambda i: (0, 0, i, 0, 0)),
        ],
        out_specs=pl.BlockSpec((2, B, B), lambda i: (i, 0, 0)),
    )(front, got)


def solution(mesh):
    return jax.shard_map(
        body,
        mesh=mesh,
        in_specs=(
            P(("row", "col", "rep"), None, None),
            P("rep", None, None, None),
            P("rep", None, None),
            P("rep", None, None),
            P("rep", None, "row", "col", None),
            P("rep", None, "col", "row", None),
            P(None, None, "row"),
            P(None, None, "col"),
            P(("row", "col"), None),
        ),
        out_specs=P(("row", "col", "rep"), None, None),
        check_vma=False,
    )
```

```python
import jax
import jax.numpy as jnp
from jax import lax
from jax.experimental import pallas as pl
from jax.experimental.pallas import tpu as pltpu
from jax.sharding import PartitionSpec as P

MESH = pl.DeviceIdType.MESH
NT = (((1,), (1,)), ((), ()))
B = 256
CH = 4
W = 16
SLOTS = 24
GS = 8
GROUPS = 3
SUBS = (0, 1, 3, 2)
ZN = 8
TABLE = 16


def main_kernel(
    tab_ref,
    u_hbm,
    lp_hbm,
    piv_hbm,
    ul_hbm,
    ll_hbm,
    out_ref,
    u_ref,
    lp_ref,
    piv_ref,
    ul_ref,
    ll_ref,
    pk,
    ug,
    ut,
    la,
    lb,
    lsel,
    lhs,
    acb,
    ctb,
    snd,
    in_s,
    a2a_s,
    a2a_r,
    ring_s,
    ring_r,
    sib_s,
    sib_r,
    a1_s,
    a1_r,
    a2_s,
    a2_r,
    b1_s,
    b1_r,
    b2_s,
    b2_r,
    shp_s,
    shp_r,
    loc_s,
):
    row = lax.axis_index("row")
    x = lax.axis_index("col")
    y = lax.axis_index("rep")
    z = row // 2
    core = row % 2

    def ydev(d):
        return (row, x, (y + d) % 4)

    def xdev(d):
        return (row, (x + d) % 4, y)

    def zdev(d):
        return (((z + d + ZN) % ZN) * 2 + core, x, y)

    sib = (z * 2 + 1 - core, x, y)

    def src_of(d):
        return ((z + d + ZN) % ZN) * 2 + core

    def rep_of(sub):
        return (y - SUBS[sub] + 4) % 4

    loads = [
        pltpu.make_async_copy(u_hbm, u_ref, in_s.at[0]),
        pltpu.make_async_copy(lp_hbm, lp_ref, in_s.at[1]),
        pltpu.make_async_copy(piv_hbm, piv_ref, in_s.at[2]),
        pltpu.make_async_copy(ul_hbm, ul_ref, in_s.at[3]),
        pltpu.make_async_copy(
            ll_hbm.at[pl.ds(pl.multiple_of(x * 64, 64), 64)], ll_ref, in_s.at[4]
        ),
    ]
    for load in loads:
        load.start()
    bar = pltpu.get_barrier_semaphore()
    partners = [ydev(1), ydev(2), ydev(3), xdev(1), xdev(2), xdev(3), zdev(1), zdev(-1), sib]
    for p in partners:
        pl.semaphore_signal(bar, inc=1, device_id=p, device_id_type=MESH)

    def remote(src, dst, ss, rs, dev):
        return pltpu.make_async_remote_copy(
            src_ref=src, dst_ref=dst, send_sem=ss, recv_sem=rs, device_id=dev, device_id_type=MESH
        )

    def pack(ch):
        tile = 128 * (ch // 2)
        first = 64 * (ch % 2)
        parts = [
            u_ref[:, :, j, :, tile : tile + 128].reshape(2 * GROUPS * 16, 128) for j in range(GS)
        ]
        for yy in range(4):
            at = first + W * yy
            piece = jnp.concatenate([p[:, at : at + W] for p in parts], axis=1)
            pk[ch, yy] = piece.reshape(2, GROUPS, 16, 128)
        ug[ch, row, 0] = pk[ch, y]

    def a2a(ch, sub, receive=False):
        d = SUBS[sub]
        sems = (a2a_s.at[ch, sub - 1], a2a_r.at[ch, sub - 1], ydev(d))
        ref = ug.at[ch, row, sub]
        return remote(ref if receive else pk.at[ch, (y + d) % 4], ref, *sems)

    def ring(ch, way, step, half, receive=False):
        sign = 1 if way == 0 else -1
        origin = src_of(-sign * (step + 1 if receive else step))
        ref = ug.at[ch, origin, pl.ds(2 * half, 2)]
        return remote(
            ref, ref, ring_s.at[ch, way, step, half], ring_r.at[ch, way, step, half], zdev(sign)
        )

    def sibling(ch, d, receive=False):
        s = (z + d + ZN) % ZN
        ref = ug.at[ch, s * 2 + (1 - core if receive else core)]
        return remote(ref, ref, sib_s.at[ch, d % ZN], sib_r.at[ch, d % ZN], sib)

    def goes(way, step, half):
        return step < 3 or half == way

    def ring_step(ch, step):
        for half in range(2):
            if step == 0:
                for sub in (1,) if half == 0 else (2, 3):
                    a2a(ch, sub, True).wait_recv()
            for way in range(2):
                if step and goes(way, step - 1, half):
                    ring(ch, way, step - 1, half, True).wait_recv()
                if step < 4 and goes(way, step, half):
                    ring(ch, way, step, half).start()
        if step in (0, 4):
            sibling(ch, step).start()
        else:
            sibling(ch, -step).start()
            sibling(ch, step).start()

    def wait_sibling(ch):
        for d in range(ZN):
            sibling(ch, d, True).wait_recv()

    def a_first(d, receive=False):
        ref = la.at[0, (x - d + 4) % 4 if receive else x, pl.ds(0, 2)]
        return remote(ref, ref, a1_s.at[d - 1], a1_r.at[d - 1], xdev(d))

    def a_next(e, sub, receive=False):
        xx = (x - e + 4) % 4
        dst = la.at[sub, xx, pl.ds(0, 2)]
        src = dst if receive else la.at[0, xx, pl.ds(0, 2)]
        return remote(src, dst, a2_s.at[e, sub - 1], a2_r.at[e, sub - 1], ydev(SUBS[sub]))

    def b_first(sub, receive=False):
        dst = lb.at[sub, x, pl.ds(0, 3)]
        src = dst if receive else lb.at[0, x, pl.ds(0, 3)]
        return remote(src, dst, b1_s.at[sub - 1], b1_r.at[sub - 1], ydev(SUBS[sub]))

    def b_next(sub, d, receive=False):
        ref = lb.at[sub, (x - d + 4) % 4 if receive else x, pl.ds(0, 3)]
        return remote(ref, ref, b2_s.at[sub, d - 1], b2_r.at[sub, d - 1], xdev(d))

    def ship(ch, d, receive=False):
        dst = out_ref.at[ch, (y - d + 4) % 4 if receive else y]
        src = dst if receive else snd.at[ch, (y + d) % 4]
        return remote(src, dst, shp_s.at[ch, d - 1], shp_r.at[ch, d - 1], ydev(d))

    def lower_prep():
        first = jnp.dot(
            lp_ref[0].reshape(128, B), piv_ref[0], preferred_element_type=jnp.float32
        ).astype(jnp.bfloat16)
        la[0, x, 0:2] = first.reshape(2, 64, B)
        for d in (1, 3, 2):
            a_first(d).start()
        link = jnp.dot(ll_ref[...], piv_ref[0], preferred_element_type=jnp.float32)
        lb[0, x, 2] = link.astype(jnp.bfloat16)
        wide = first.astype(jnp.float32)
        pieces = []
        for g in range(2):
            sg = tab_ref[12, 4 * y + 2 + g]
            hit0 = jnp.where((sg >= 0) & (sg == tab_ref[12, 4 * y]), 1.0, 0.0)
            hit1 = jnp.where((sg >= 0) & (sg == tab_ref[12, 4 * y + 1]), 1.0, 0.0)
            pieces.append(wide[:64] * hit0 + wide[64:] * hit1)
        carried = jnp.concatenate(pieces, axis=0).astype(jnp.bfloat16)
        term = jnp.dot(carried, ul_ref[...], preferred_element_type=jnp.float32)
        diff = (lp_ref[1].reshape(128, B).astype(jnp.float32) - term).astype(jnp.bfloat16)
        second = jnp.dot(diff, piv_ref[1], preferred_element_type=jnp.float32).astype(jnp.bfloat16)
        lb[0, x, 0:2] = second.reshape(2, 64, B)
        for sub in (1, 2, 3):
            b_first(sub).start()

    def lower_forward():
        for d in (1, 3, 2):
            b_next(0, d).start()
        for sub in (1, 2, 3):
            a_next(0, sub).start()
        for i in range(3):
            sub, e = i + 1, (1, 3, 2)[i]
            b_first(sub, True).wait_recv()
            for d in (1, 3, 2):
                b_next(sub, d).start()
            a_first(e, True).wait_recv()
            for s in (1, 2, 3):
                a_next(e, s).start()

    def lower_select():
        for e in range(4):
            for s in (1, 2, 3):
                a_next(e, s, True).wait_recv()
        for s in range(4):
            for d in (1, 2, 3):
                b_next(s, d, True).wait_recv()
        for s in range(4):
            q = rep_of(s)
            for k, store in ((0, la), (1, lb)):
                s0 = tab_ref[12, 4 * q + 2 * k]
                s1 = tab_ref[12, 4 * q + 2 * k + 1]
                for a in range(2):
                    at = jnp.where(s0 == a, 0, jnp.where(s1 == a, 1, 2 + k))
                    for xx in range(4):
                        lsel[a, xx * 64 : xx * 64 + 64, (2 * s + k) * B : (2 * s + k + 1) * B] = (
                            store[s, xx, at]
                        )

    def turn(ch):
        def step(i, carry):
            s, k = i // 2, i % 2
            for g in range(GROUPS):
                block = ug[ch, :, s, k, g].reshape(B, 128)
                ut[s, k, GS * g : GS * g + GS] = block.T.reshape(GS, W, B)
            return carry

        lax.fori_loop(0, 8, step, 0)

    def arrange():
        def step(b, carry):
            rows = pl.ds(pl.multiple_of(b * W, W), W)
            for s in range(4):
                q = rep_of(s)
                lhs[rows, 2 * s * B : 2 * s * B + B] = ut[s, 0, tab_ref[q * 3, b]]
                lhs[rows, (2 * s + 1) * B : (2 * s + 2) * B] = ut[s, 1, tab_ref[q * 3 + 1, b]]
                acb[s, rows, :] = ut[s, 0, tab_ref[q * 3 + 2, b]]
            return carry

        lax.fori_loop(0, 32, step, 0)

    def second_upper():
        for s in range(4):
            link = lb[s, :, 2].reshape(B, B)
            shift = lax.dot_general(acb[s], link, NT, preferred_element_type=jnp.float32)
            cols = slice((2 * s + 1) * B, (2 * s + 2) * B)
            lhs[:, cols] = (lhs[:, cols].astype(jnp.float32) - shift).astype(jnp.bfloat16)

    def multiply():
        for a in range(2):
            prod = lax.dot_general(lhs[...], lsel[a], NT, preferred_element_type=jnp.float32)
            ctb[a] = prod.astype(jnp.bfloat16).reshape(32, W, B)

    def choose(ch):
        def step(i, carry):
            for j in range(4):
                e = tab_ref[13 + i // 8, (i % 8) * 4 + j]
                snd[ch, i // 4, (i % 4) * 4 + j] = ctb[e // 32, e % 32]
            return carry

        lax.fori_loop(0, 16, step, 0)

    def local_out(ch):
        return pltpu.make_async_copy(snd.at[ch, y], out_ref.at[ch, y], loc_s.at[ch])

    def p1(ch):
        wait_sibling(ch)
        turn(ch)

    def p2():
        arrange()
        second_upper()

    def p4(ch):
        choose(ch)
        for d in (1, 3, 2):
            ship(ch, d).start()
        local_out(ch).start()

    for s in range(4):
        for k in range(2):
            ut[s, k, SLOTS] = jnp.zeros((W, B), jnp.bfloat16)
        for xx in range(4):
            la[s, xx, 2] = jnp.zeros((64, B), jnp.bfloat16)
            lb[s, xx, 3] = jnp.zeros((64, B), jnp.bfloat16)
    loads[0].wait()
    pack(0)
    pl.semaphore_wait(bar, len(partners))
    for sub in (1, 2, 3):
        a2a(0, sub).start()
    pack(1)
    for sub in (1, 2, 3):
        a2a(1, sub).start()
    for load in loads[1:]:
        load.wait()
    lower_prep()
    ring_step(0, 0)
    for ch in (2, 3):
        pack(ch)
        for sub in (1, 2, 3):
            a2a(ch, sub).start()
        if ch == 2:
            ring_step(0, 1)
    ring_step(1, 0)
    lower_forward()
    ring_step(0, 2)
    ring_step(1, 1)
    ring_step(0, 3)
    ring_step(2, 0)
    ring_step(0, 4)
    ring_step(1, 2)
    p1(0)
    ring_step(2, 1)
    lower_select()
    p2()
    ring_step(1, 3)
    multiply()
    ring_step(3, 0)
    p4(0)
    ring_step(1, 4)
    ring_step(2, 2)
    p1(1)
    ring_step(3, 1)
    p2()
    ring_step(2, 3)
    multiply()
    ring_step(3, 2)
    p4(1)
    ring_step(2, 4)
    ring_step(3, 3)
    p1(2)
    p2()
    ring_step(3, 4)
    multiply()
    p4(2)
    p1(3)
    p2()
    multiply()
    p4(3)

    for ch in range(CH):
        for sub in (1, 2, 3):
            a2a(ch, sub).wait_send()
        for way in range(2):
            for step in range(4):
                for half in range(2):
                    if goes(way, step, half):
                        ring(ch, way, step, half).wait_send()
        for d in range(ZN):
            sibling(ch, d).wait_send()
    for i in range(4):
        for d in (1, 2, 3):
            a_next(i, d).wait_send()
            b_next(i, d).wait_send()
            if i == 0:
                a_first(d).wait_send()
                b_first(d).wait_send()
    for ch in range(CH):
        local_out(ch).wait()
        for d in (1, 2, 3):
            ship(ch, d).wait_send()
            ship(ch, d, True).wait_recv()


def finish_kernel(front_hbm, got_hbm, out_hbm, front, got, out, front_s, got_s, out_s):
    got_copies = [
        pltpu.make_async_copy(
            got_hbm.at[:, :, pl.ds(4 * i, 4)], got.at[:, :, pl.ds(4 * i, 4)], got_s.at[i]
        )
        for i in range(4)
    ]

    def fetch(i):
        return pltpu.make_async_copy(front_hbm.at[i], front.at[i], front_s.at[i])

    def store(i):
        return pltpu.make_async_copy(out.at[i], out_hbm.at[i], out_s.at[i])

    for i in range(16):
        if i % 4 == 0:
            got_copies[i // 4].start()
        fetch(i).start()
    for i in range(16):
        if i % 4 == 0:
            got_copies[i // 4].wait()
        fetch(i).wait()
        block = got[:, :, i].reshape(B, B)
        out[i] = front[i] - block.T.astype(jnp.float32)
        store(i).start()
    for i in range(16):
        store(i).wait()


def body(
    front,
    pivots,
    upper_link,
    lower_link,
    lower_panels,
    upper_panels,
    lower_slots,
    upper_slots,
    owner_map,
):
    names = jnp.arange(32, dtype=jnp.int32)
    same = upper_slots[:, :, None, :] == names[None, None, :, None]
    at = jnp.arange(SLOTS, dtype=jnp.int32)
    inv = jnp.min(jnp.where(same, at[None, None, None, :], SLOTS), axis=-1)
    carried = jnp.where(inv[:, 1] < SLOTS, inv[:, 0], SLOTS)
    inv = jnp.concatenate([inv, carried[:, None]], axis=1).reshape(12, 32)
    low = jnp.pad(lower_slots.reshape(1, 16), ((0, 0), (0, 16)))
    table = jnp.concatenate([inv, low, owner_map.reshape(2, 32)], axis=0)
    table = jnp.pad(table, ((0, TABLE - 15), (0, 0)))
    smem = pl.BlockSpec(memory_space=pltpu.SMEM)
    hbm = pl.BlockSpec(memory_space=pl.ANY)
    dma = pltpu.SemaphoreType.DMA
    bf = jnp.bfloat16
    got = pl.pallas_call(
        main_kernel,
        out_shape=jax.ShapeDtypeStruct((CH, 4, 16, W, B), bf),
        in_specs=[smem] + [hbm] * 5,
        out_specs=hbm,
        scratch_shapes=[
            pltpu.VMEM((2, GROUPS, GS, 16, B), bf),
            pltpu.VMEM((2, 2, 64, B), bf),
            pltpu.VMEM((2, B, B), bf),
            pltpu.VMEM((B, B), bf),
            pltpu.VMEM((64, B), bf),
            pltpu.VMEM((CH, 4, 2, GROUPS, 16, 128), bf),
            pltpu.VMEM((CH, 16, 4, 2, GROUPS, 16, 128), bf),
            pltpu.VMEM((4, 2, SLOTS + 1, W, B), bf),
            pltpu.VMEM((4, 4, 3, 64, B), bf),
            pltpu.VMEM((4, 4, 4, 64, B), bf),
            pltpu.VMEM((2, B, 8 * B), bf),
            pltpu.VMEM((32 * W, 8 * B), bf),
            pltpu.VMEM((4, 32 * W, B), bf),
            pltpu.VMEM((2, 32, W, B), bf),
            pltpu.VMEM((CH, 4, 16, W, B), bf),
            dma((5,)),
            dma((CH, 3)),
            dma((CH, 3)),
            dma((CH, 2, 4, 2)),
            dma((CH, 2, 4, 2)),
            dma((CH, ZN)),
            dma((CH, ZN)),
            dma((3,)),
            dma((3,)),
            dma((4, 3)),
            dma((4, 3)),
            dma((3,)),
            dma((3,)),
            dma((4, 3)),
            dma((4, 3)),
            dma((CH, 3)),
            dma((CH, 3)),
            dma((CH,)),
        ],
        compiler_params=pltpu.CompilerParams(
            collective_id=0, has_side_effects=True, vmem_limit_bytes=60 << 20
        ),
    )(
        table,
        upper_panels[0].reshape(2, GROUPS, GS, 16, B),
        lower_panels[0],
        pivots[0],
        upper_link[0],
        lower_link[0],
    )
    return pl.pallas_call(
        finish_kernel,
        out_shape=jax.ShapeDtypeStruct(front.shape, front.dtype),
        in_specs=[hbm, hbm],
        out_specs=hbm,
        scratch_shapes=[
            pltpu.VMEM((16, B, B), jnp.float32),
            pltpu.VMEM((CH, 4, 16, W, B), bf),
            pltpu.VMEM((16, B, B), jnp.float32),
            dma((16,)),
            dma((4,)),
            dma((16,)),
        ],
        compiler_params=pltpu.CompilerParams(vmem_limit_bytes=60 << 20),
    )(front, got)


def solution(mesh):
    return jax.shard_map(
        body,
        mesh=mesh,
        in_specs=(
            P(("row", "col", "rep"), None, None),
            P("rep", None, None, None),
            P("rep", None, None),
            P("rep", None, None),
            P("rep", None, "row", "col", None),
            P("rep", None, "col", "row", None),
            P(None, None, "row"),
            P(None, None, "col"),
            P(("row", "col"), None),
        ),
        out_specs=P(("row", "col", "rep"), None, None),
        check_vma=False,
    )
```

```python
import jax
import jax.numpy as jnp
from jax import lax
from jax.experimental import pallas as pl
from jax.experimental.pallas import tpu as pltpu
from jax.sharding import PartitionSpec as P

MESH = pl.DeviceIdType.MESH
NT = (((1,), (1,)), ((), ()))
B = 256
CH = 4
W = 16
SLOTS = 24
GS = 8
GROUPS = 3
PIECE = 2 * GROUPS * 16
SUBS = (0, 1, 3, 2)
ZN = 8
EVENTS = (
    ("0", 0),
    ("a2a", 2),
    ("0", 1),
    ("a2a", 3),
    ("1", 0),
    ("forward", 0),
    ("1", 1),
    ("2", 0),
    ("0", 2),
    ("2", 1),
    ("3", 0),
    ("1", 2),
    ("4", 0),
    ("0", 3),
    ("p1", 0),
    ("3", 1),
    ("2", 2),
    ("select", 0),
    ("p2", 0),
    ("4", 1),
    ("1", 3),
    ("p3", 0),
    ("p4", 0),
    ("3", 2),
    ("p1", 1),
    ("p2", 0),
    ("2", 3),
    ("p3", 0),
    ("p4", 1),
    ("4", 2),
    ("3", 3),
    ("p1", 2),
    ("p2", 0),
    ("4", 3),
    ("p3", 0),
    ("p4", 2),
    ("p1", 3),
    ("p2", 0),
    ("p3", 0),
    ("p4", 3),
)


def main_kernel(
    tab_ref,
    low_ref,
    own_ref,
    u_hbm,
    lp_hbm,
    piv_hbm,
    ul_hbm,
    ll_hbm,
    out_ref,
    u_ref,
    lp_ref,
    piv_ref,
    ul_ref,
    ll_ref,
    pk,
    ug,
    ut,
    la,
    lb,
    lsel,
    lhs,
    acb,
    ctb,
    snd,
    in_s,
    a2a_s,
    a2a_r,
    ring_s,
    ring_r,
    sib_s,
    sib_r,
    both_s,
    both_r,
    a1_s,
    a1_r,
    a2_s,
    a2_r,
    b1_s,
    b1_r,
    b2_s,
    b2_r,
    shp_s,
    shp_r,
    loc_s,
):
    row = lax.axis_index("row")
    x = lax.axis_index("col")
    y = lax.axis_index("rep")
    z = row // 2
    core = row % 2

    def ydev(d):
        return (row, x, (y + d) % 4)

    def xdev(d):
        return (row, (x + d) % 4, y)

    def zdev(d):
        return (((z + d + ZN) % ZN) * 2 + core, x, y)

    sib = (z * 2 + 1 - core, x, y)

    def src_of(d):
        return ((z + d + ZN) % ZN) * 2 + core

    def rep_of(sub):
        return (y - SUBS[sub] + 4) % 4

    loads = [
        pltpu.make_async_copy(u_hbm, u_ref, in_s.at[0]),
        pltpu.make_async_copy(lp_hbm, lp_ref, in_s.at[1]),
        pltpu.make_async_copy(piv_hbm, piv_ref, in_s.at[2]),
        pltpu.make_async_copy(ul_hbm, ul_ref, in_s.at[3]),
        pltpu.make_async_copy(
            ll_hbm.at[pl.ds(pl.multiple_of(x * 64, 64), 64)], ll_ref, in_s.at[4]
        ),
    ]
    for load in loads:
        load.start()
    bar = pltpu.get_barrier_semaphore()
    partners = [ydev(1), ydev(2), ydev(3), xdev(1), xdev(2), xdev(3), zdev(1), zdev(-1), sib]
    partners += [(((z + d + ZN) % ZN) * 2 + 1 - core, x, y) for d in (1, -1)]
    for p in partners:
        pl.semaphore_signal(bar, inc=1, device_id=p, device_id_type=MESH)

    def remote(src, dst, ss, rs, dev):
        return pltpu.make_async_remote_copy(
            src_ref=src, dst_ref=dst, send_sem=ss, recv_sem=rs, device_id=dev, device_id_type=MESH
        )

    def pack(ch):
        tile = 128 * (ch // 2)
        first = 64 * (ch % 2)
        parts = [
            u_ref[:, :, j, :, tile : tile + 128].reshape(2 * GROUPS * 16, 128) for j in range(GS)
        ]
        for yy in range(4):
            at = first + W * yy
            piece = jnp.concatenate([p[:, at : at + W] for p in parts], axis=1)
            pk[ch, yy] = piece
        ug[ch, row, 0:PIECE] = pk[ch, y]

    def a2a(ch, sub, receive=False):
        d = SUBS[sub]
        sems = (a2a_s.at[ch, sub - 1], a2a_r.at[ch, sub - 1], ydev(d))
        ref = ug.at[ch, row, pl.ds(sub * PIECE, PIECE)]
        return remote(ref if receive else pk.at[ch, (y + d) % 4], ref, *sems)

    def ring(ch, way, step, half, receive=False):
        sign = 1 if way == 0 else -1
        origin = src_of(-sign * (step + 1 if receive else step))
        if step == 0:
            ref = ug.at[ch, origin, pl.ds(half * PIECE, PIECE)]
        else:
            ref = ug.at[ch, origin, pl.ds(2 * half * PIECE, 2 * PIECE)]
        return remote(
            ref, ref, ring_s.at[ch, way, step, half], ring_r.at[ch, way, step, half], zdev(sign)
        )

    def both(way, receive=False):
        sign = 1 if way == 0 else -1
        hops = -sign * (4 if receive else 3)
        at = ((z + hops + ZN) % ZN) * 2 + (1 - core if receive else core)
        ref = ug.at[CH - 1, at, pl.ds(2 * way * PIECE, 2 * PIECE)]
        dev = (((z + sign + ZN) % ZN) * 2 + 1 - core, x, y)
        return remote(ref, ref, both_s.at[way], both_r.at[way], dev)

    def sibling(ch, d, receive=False):
        s = (z + d + ZN) % ZN
        ref = ug.at[ch, s * 2 + (1 - core if receive else core)]
        return remote(ref, ref, sib_s.at[ch, d % ZN], sib_r.at[ch, d % ZN], sib)

    def goes(way, step, half):
        return step < 3 or half == way

    def ring_own(ch):
        for way in range(2):
            ring(ch, way, 0, 0).start()

    def ring_step(ch, step):
        if step == 0:
            for sub in (1, 2, 3):
                a2a(ch, sub, True).wait_recv()
                for way in range(2):
                    ring(ch, way, 0, sub).start()
            sibling(ch, 0).start()
            return
        for half in range(2):
            for way in range(2):
                if step == 1:
                    ring(ch, way, 0, 2 * half, True).wait_recv()
                    ring(ch, way, 0, 2 * half + 1, True).wait_recv()
                elif goes(way, step - 1, half):
                    ring(ch, way, step - 1, half, True).wait_recv()
                if step < 4 and goes(way, step, half):
                    ring(ch, way, step, half).start()
                    if step == 3 and ch == CH - 1:
                        both(way).start()
        if step == 4:
            if ch < CH - 1:
                sibling(ch, step).start()
        else:
            sibling(ch, -step).start()
            sibling(ch, step).start()

    def wait_sibling(ch):
        for d in range(ZN):
            if d == 4 and ch == CH - 1:
                both(0, True).wait_recv()
                both(1, True).wait_recv()
            else:
                sibling(ch, d, True).wait_recv()

    def a_first(d, receive=False):
        ref = la.at[0, (x - d + 4) % 4 if receive else x, pl.ds(0, 2)]
        return remote(ref, ref, a1_s.at[d - 1], a1_r.at[d - 1], xdev(d))

    def a_next(e, sub, receive=False):
        xx = (x - e + 4) % 4
        dst = la.at[sub, xx, pl.ds(0, 2)]
        src = dst if receive else la.at[0, xx, pl.ds(0, 2)]
        return remote(src, dst, a2_s.at[e, sub - 1], a2_r.at[e, sub - 1], ydev(SUBS[sub]))

    def b_first(sub, receive=False):
        dst = lb.at[sub, x, pl.ds(0, 3)]
        src = dst if receive else lb.at[0, x, pl.ds(0, 3)]
        return remote(src, dst, b1_s.at[sub - 1], b1_r.at[sub - 1], ydev(SUBS[sub]))

    def b_next(sub, d, receive=False):
        ref = lb.at[sub, (x - d + 4) % 4 if receive else x, pl.ds(0, 3)]
        return remote(ref, ref, b2_s.at[sub, d - 1], b2_r.at[sub, d - 1], xdev(d))

    def ship(ch, d, receive=False):
        dst = out_ref.at[ch, (y - d + 4) % 4 if receive else y]
        src = dst if receive else snd.at[ch, (y + d) % 4]
        return remote(src, dst, shp_s.at[ch, d - 1], shp_r.at[ch, d - 1], ydev(d))

    def lower_prep():
        first = jnp.dot(
            lp_ref[0].reshape(128, B), piv_ref[0], preferred_element_type=jnp.float32
        ).astype(jnp.bfloat16)
        la[0, x, 0:2] = first.reshape(2, 64, B)
        for d in (1, 3, 2):
            a_first(d).start()
        link = jnp.dot(ll_ref[...], piv_ref[0], preferred_element_type=jnp.float32)
        lb[0, x, 2] = link.astype(jnp.bfloat16)
        wide = first.astype(jnp.float32)
        pieces = []
        for g in range(2):
            sg = low_ref[2 + g, y]
            hit0 = jnp.where((sg >= 0) & (sg == low_ref[0, y]), 1.0, 0.0)
            hit1 = jnp.where((sg >= 0) & (sg == low_ref[1, y]), 1.0, 0.0)
            pieces.append(wide[:64] * hit0 + wide[64:] * hit1)
        carried = jnp.concatenate(pieces, axis=0).astype(jnp.bfloat16)
        term = jnp.dot(carried, ul_ref[...], preferred_element_type=jnp.float32)
        diff = (lp_ref[1].reshape(128, B).astype(jnp.float32) - term).astype(jnp.bfloat16)
        second = jnp.dot(diff, piv_ref[1], preferred_element_type=jnp.float32).astype(jnp.bfloat16)
        lb[0, x, 0:2] = second.reshape(2, 64, B)
        for sub in (1, 2, 3):
            b_first(sub).start()

    def lower_forward():
        for d in (1, 3, 2):
            b_next(0, d).start()
        for sub in (1, 2, 3):
            a_next(0, sub).start()
        for i in range(3):
            sub, e = i + 1, (1, 3, 2)[i]
            b_first(sub, True).wait_recv()
            for d in (1, 3, 2):
                b_next(sub, d).start()
            a_first(e, True).wait_recv()
            for s in (1, 2, 3):
                a_next(e, s).start()

    def lower_select():
        for e in range(4):
            for s in (1, 2, 3):
                a_next(e, s, True).wait_recv()
        for s in range(4):
            for d in (1, 2, 3):
                b_next(s, d, True).wait_recv()
        for s in range(4):
            q = rep_of(s)
            for k, store in ((0, la), (1, lb)):
                s0 = low_ref[2 * k, q]
                s1 = low_ref[2 * k + 1, q]
                for a in range(2):
                    at = jnp.where(s0 == a, 0, jnp.where(s1 == a, 1, 2 + k))
                    for xx in range(4):
                        lsel[a, xx * 64 : xx * 64 + 64, (2 * s + k) * B : (2 * s + k + 1) * B] = (
                            store[s, xx, at]
                        )

    def turn(ch):
        def step(i, carry):
            s, k = i // 2, i % 2
            for g in range(GROUPS):
                rows = pl.ds(pl.multiple_of((i * GROUPS + g) * 16, 16), 16)
                block = ug[ch, :, rows, :].reshape(B, 128)
                ut[s, k, GS * g : GS * g + GS] = block.T.reshape(GS, W, B)
            return carry

        lax.fori_loop(0, 8, step, 0)

    def arrange():
        def step(b, carry):
            rows = pl.ds(pl.multiple_of(b * W, W), W)
            for s in range(4):
                q = rep_of(s)
                lhs[rows, 2 * s * B : 2 * s * B + B] = ut[s, 0, tab_ref[q * 3, b]]
                lhs[rows, (2 * s + 1) * B : (2 * s + 2) * B] = ut[s, 1, tab_ref[q * 3 + 1, b]]
                acb[s, rows, :] = ut[s, 0, tab_ref[q * 3 + 2, b]]
            return carry

        lax.fori_loop(0, 32, step, 0)

    def second_upper():
        for s in range(4):
            link = lb[s, :, 2].reshape(B, B)
            shift = lax.dot_general(acb[s], link, NT, preferred_element_type=jnp.float32)
            cols = slice((2 * s + 1) * B, (2 * s + 2) * B)
            lhs[:, cols] = (lhs[:, cols].astype(jnp.float32) - shift).astype(jnp.bfloat16)

    def multiply():
        for a in range(2):
            prod = lax.dot_general(lhs[...], lsel[a], NT, preferred_element_type=jnp.float32)
            ctb[32 * a : 32 * a + 32] = prod.astype(jnp.bfloat16).reshape(32, W, B)

    def choose(ch):
        def step(i, carry):
            for j in range(4):
                e = own_ref[0, i * 4 + j]
                rows = pl.ds(pl.multiple_of(((i % 4) * 4 + j) * W, W), W)
                snd[ch, i // 4, rows, :] = ctb[e]
            return carry

        lax.fori_loop(0, 16, step, 0)

    def local_out(ch):
        return pltpu.make_async_copy(snd.at[ch, y], out_ref.at[ch, y], loc_s.at[ch])

    def p1(ch):
        wait_sibling(ch)
        turn(ch)

    def p2():
        arrange()
        second_upper()

    def p4(ch):
        choose(ch)
        for d in (1, 3, 2):
            ship(ch, d).start()
        local_out(ch).start()

    def zero_fill():
        for s in range(4):
            for k in range(2):
                ut[s, k, SLOTS] = jnp.zeros((W, B), jnp.bfloat16)
            for xx in range(4):
                la[s, xx, 2] = jnp.zeros((64, B), jnp.bfloat16)
                lb[s, xx, 3] = jnp.zeros((64, B), jnp.bfloat16)

    def a2a_start(ch):
        for sub in (1, 2, 3):
            a2a(ch, sub).start()

    loads[0].wait()
    pack(0)
    pl.semaphore_wait(bar, len(partners))
    a2a_start(0)
    ring_own(0)
    pack(1)
    a2a_start(1)
    ring_own(1)
    for ch in (2, 3):
        pack(ch)
        ring_own(ch)
    for load in loads[1:]:
        load.wait()
    lower_prep()
    for what, ch in EVENTS:
        if what == "a2a":
            a2a_start(ch)
        elif what == "forward":
            zero_fill()
            lower_forward()
        elif what == "select":
            lower_select()
        elif what == "p1":
            p1(ch)
        elif what == "p2":
            p2()
        elif what == "p3":
            multiply()
        elif what == "p4":
            p4(ch)
        else:
            ring_step(ch, int(what))

    for ch in range(CH):
        for sub in (1, 2, 3):
            a2a(ch, sub).wait_send()
        for way in range(2):
            for step in range(4):
                for half in range(2 if step else 4):
                    if goes(way, step, half):
                        ring(ch, way, step, half).wait_send()
        for d in range(ZN):
            if d == 4 and ch == CH - 1:
                both(0).wait_send()
                both(1).wait_send()
            else:
                sibling(ch, d).wait_send()
    for i in range(4):
        for d in (1, 2, 3):
            a_next(i, d).wait_send()
            b_next(i, d).wait_send()
            if i == 0:
                a_first(d).wait_send()
                b_first(d).wait_send()
    for ch in range(CH):
        local_out(ch).wait()
        for d in (1, 2, 3):
            ship(ch, d).wait_send()
            ship(ch, d, True).wait_recv()


def finish_kernel(front_hbm, got_hbm, out_hbm, front, got, out, front_s, got_s, out_s):
    got_copies = [
        pltpu.make_async_copy(
            got_hbm.at[:, :, pl.ds(4 * W * i, 4 * W)],
            got.at[:, :, pl.ds(4 * W * i, 4 * W)],
            got_s.at[i],
        )
        for i in range(4)
    ]

    def fetch(i):
        return pltpu.make_async_copy(front_hbm.at[i], front.at[i], front_s.at[i])

    def store(i):
        return pltpu.make_async_copy(out.at[i], out_hbm.at[i], out_s.at[i])

    for i in range(16):
        if i % 4 == 0:
            got_copies[i // 4].start()
        fetch(i).start()
    for i in range(16):
        if i % 4 == 0:
            got_copies[i // 4].wait()
        fetch(i).wait()
        block = got[:, :, W * i : W * i + W].reshape(B, B)
        out[i] = front[i] - block.T.astype(jnp.float32)
        store(i).start()
    for i in range(16):
        store(i).wait()


def body(
    front,
    pivots,
    upper_link,
    lower_link,
    lower_panels,
    upper_panels,
    lower_slots,
    upper_slots,
    owner_map,
):
    names = jnp.arange(32, dtype=jnp.int32)
    same = upper_slots[:, :, None, :] == names[None, None, :, None]
    at = jnp.arange(SLOTS, dtype=jnp.int32)
    inv = jnp.min(jnp.where(same, at[None, None, None, :], SLOTS), axis=-1)
    carried = jnp.where(inv[:, 1] < SLOTS, inv[:, 0], SLOTS)
    inv = jnp.concatenate([inv, carried[:, None]], axis=1).reshape(12, 32)
    smem = pl.BlockSpec(memory_space=pltpu.SMEM)
    hbm = pl.BlockSpec(memory_space=pl.ANY)
    dma = pltpu.SemaphoreType.DMA
    bf = jnp.bfloat16
    got = pl.pallas_call(
        main_kernel,
        out_shape=jax.ShapeDtypeStruct((CH, 4, 16 * W, B), bf),
        in_specs=[smem] * 3 + [hbm] * 5,
        out_specs=hbm,
        scratch_shapes=[
            pltpu.VMEM((2, GROUPS, GS, 16, B), bf),
            pltpu.VMEM((2, 2, 64, B), bf),
            pltpu.VMEM((2, B, B), bf),
            pltpu.VMEM((B, B), bf),
            pltpu.VMEM((64, B), bf),
            pltpu.VMEM((CH, 4, PIECE, 128), bf),
            pltpu.VMEM((CH, 16, 4 * PIECE, 128), bf),
            pltpu.VMEM((4, 2, SLOTS + 1, W, B), bf),
            pltpu.VMEM((4, 4, 3, 64, B), bf),
            pltpu.VMEM((4, 4, 4, 64, B), bf),
            pltpu.VMEM((2, B, 8 * B), bf),
            pltpu.VMEM((32 * W, 8 * B), bf),
            pltpu.VMEM((4, 32 * W, B), bf),
            pltpu.VMEM((64, W, B), bf),
            pltpu.VMEM((CH, 4, 16 * W, B), bf),
            dma((5,)),
            dma((CH, 3)),
            dma((CH, 3)),
            dma((CH, 2, 4, 4)),
            dma((CH, 2, 4, 4)),
            dma((CH, ZN)),
            dma((CH, ZN)),
            dma((2,)),
            dma((2,)),
            dma((3,)),
            dma((3,)),
            dma((4, 3)),
            dma((4, 3)),
            dma((3,)),
            dma((3,)),
            dma((4, 3)),
            dma((4, 3)),
            dma((CH, 3)),
            dma((CH, 3)),
            dma((CH,)),
        ],
        compiler_params=pltpu.CompilerParams(
            collective_id=0, has_side_effects=True, vmem_limit_bytes=60 << 20
        ),
    )(
        inv,
        jnp.transpose(lower_slots, (1, 2, 0)).reshape(4, 4),
        owner_map,
        upper_panels[0].reshape(2, GROUPS, GS, 16, B),
        lower_panels[0],
        pivots[0],
        upper_link[0],
        lower_link[0],
    )
    return pl.pallas_call(
        finish_kernel,
        out_shape=jax.ShapeDtypeStruct(front.shape, front.dtype),
        in_specs=[hbm, hbm],
        out_specs=hbm,
        scratch_shapes=[
            pltpu.VMEM((16, B, B), jnp.float32),
            pltpu.VMEM((CH, 4, 16 * W, B), bf),
            pltpu.VMEM((16, B, B), jnp.float32),
            dma((16,)),
            dma((4,)),
            dma((16,)),
        ],
        compiler_params=pltpu.CompilerParams(vmem_limit_bytes=60 << 20),
    )(front, got)


def solution(mesh):
    return jax.shard_map(
        body,
        mesh=mesh,
        in_specs=(
            P(("row", "col", "rep"), None, None),
            P("rep", None, None, None),
            P("rep", None, None),
            P("rep", None, None),
            P("rep", None, "row", "col", None),
            P("rep", None, "col", "row", None),
            P(None, None, "row"),
            P(None, None, "col"),
            P(("row", "col"), None),
        ),
        out_specs=P(("row", "col", "rep"), None, None),
        check_vma=False,
    )
```

```python
import jax
import jax.numpy as jnp
from jax import lax
from jax.experimental import pallas as pl
from jax.experimental.pallas import tpu as pltpu
from jax.sharding import PartitionSpec as P

MESH = pl.DeviceIdType.MESH
NT = (((1,), (1,)), ((), ()))
B = 256
CH = 4
W = 16
SLOTS = 24
GS = 8
GROUPS = 3
PIECE = 2 * GROUPS * 16
SUBS = (0, 1, 3, 2)
ZN = 8
EVENTS = (
    ("0", 0),
    ("a2a", 2),
    ("0", 1),
    ("a2a", 3),
    ("1", 0),
    ("1", 1),
    ("forward", 0),
    ("2", 0),
    ("0", 2),
    ("2", 1),
    ("3", 0),
    ("1", 2),
    ("4", 0),
    ("0", 3),
    ("p1", 0),
    ("3", 1),
    ("2", 2),
    ("select", 0),
    ("p2", 0),
    ("4", 1),
    ("1", 3),
    ("p3", 0),
    ("p4", 0),
    ("3", 2),
    ("p1", 1),
    ("p2", 0),
    ("2", 3),
    ("p3", 0),
    ("p4", 1),
    ("4", 2),
    ("3", 3),
    ("p1", 2),
    ("p2", 0),
    ("4", 3),
    ("p3", 0),
    ("p4", 2),
    ("p1", 3),
    ("p2", 0),
    ("p3", 0),
    ("p4", 3),
)


def main_kernel(
    low_ref,
    own_ref,
    slots_hbm,
    u_hbm,
    lp_hbm,
    piv_hbm,
    ul_hbm,
    ll_hbm,
    out_ref,
    slots_ref,
    tab_vmem,
    tab_ref,
    u_ref,
    lp_ref,
    piv_ref,
    ul_ref,
    ll_ref,
    pk,
    ug,
    ut,
    la,
    lb,
    lsel,
    lhs,
    acb,
    ctb,
    snd,
    in_s,
    a2a_s,
    a2a_r,
    ring_s,
    ring_r,
    sib_s,
    sib_r,
    both_s,
    both_r,
    a1_s,
    a1_r,
    a2_s,
    a2_r,
    b1_s,
    b1_r,
    b2_s,
    b2_r,
    shp_s,
    shp_r,
    loc_s,
):
    row = lax.axis_index("row")
    x = lax.axis_index("col")
    y = lax.axis_index("rep")
    z = row // 2
    core = row % 2

    def ydev(d):
        return (row, x, (y + d) % 4)

    def xdev(d):
        return (row, (x + d) % 4, y)

    def zdev(d):
        return (((z + d + ZN) % ZN) * 2 + core, x, y)

    sib = (z * 2 + 1 - core, x, y)

    def src_of(d):
        return ((z + d + ZN) % ZN) * 2 + core

    def rep_of(sub):
        return (y - SUBS[sub] + 4) % 4

    loads = [
        pltpu.make_async_copy(u_hbm, u_ref, in_s.at[0]),
        pltpu.make_async_copy(lp_hbm, lp_ref, in_s.at[1]),
        pltpu.make_async_copy(piv_hbm, piv_ref, in_s.at[2]),
        pltpu.make_async_copy(ul_hbm, ul_ref, in_s.at[3]),
        pltpu.make_async_copy(
            ll_hbm.at[pl.ds(pl.multiple_of(x * 64, 64), 64)], ll_ref, in_s.at[4]
        ),
    ]
    loads.append(pltpu.make_async_copy(slots_hbm, slots_ref, in_s.at[5]))
    for load in loads:
        load.start()
    bar = pltpu.get_barrier_semaphore()
    partners = [ydev(1), ydev(2), ydev(3), xdev(1), xdev(2), xdev(3), zdev(1), zdev(-1), sib]
    partners += [(((z + d + ZN) % ZN) * 2 + 1 - core, x, y) for d in (1, -1)]
    for p in partners:
        pl.semaphore_signal(bar, inc=1, device_id=p, device_id_type=MESH)

    def remote(src, dst, ss, rs, dev):
        return pltpu.make_async_remote_copy(
            src_ref=src, dst_ref=dst, send_sem=ss, recv_sem=rs, device_id=dev, device_id_type=MESH
        )

    def pack(ch):
        tile = 128 * (ch // 2)
        first = 64 * (ch % 2)
        parts = [
            u_ref[:, :, j, :, tile : tile + 128].reshape(2 * GROUPS * 16, 128) for j in range(GS)
        ]
        for yy in range(4):
            at = first + W * yy
            piece = jnp.concatenate([p[:, at : at + W] for p in parts], axis=1)
            pk[ch, yy] = piece
        ug[ch, row, 0:PIECE] = pk[ch, y]

    def a2a(ch, sub, receive=False):
        d = SUBS[sub]
        sems = (a2a_s.at[ch, sub - 1], a2a_r.at[ch, sub - 1], ydev(d))
        ref = ug.at[ch, row, pl.ds(sub * PIECE, PIECE)]
        return remote(ref if receive else pk.at[ch, (y + d) % 4], ref, *sems)

    def ring(ch, way, step, half, receive=False):
        sign = 1 if way == 0 else -1
        origin = src_of(-sign * (step + 1 if receive else step))
        if step == 0:
            ref = ug.at[ch, origin, pl.ds(half * PIECE, PIECE)]
        else:
            ref = ug.at[ch, origin, pl.ds(2 * half * PIECE, 2 * PIECE)]
        return remote(
            ref, ref, ring_s.at[ch, way, step, half], ring_r.at[ch, way, step, half], zdev(sign)
        )

    def both(way, receive=False):
        sign = 1 if way == 0 else -1
        hops = -sign * (4 if receive else 3)
        at = ((z + hops + ZN) % ZN) * 2 + (1 - core if receive else core)
        ref = ug.at[CH - 1, at, pl.ds(2 * way * PIECE, 2 * PIECE)]
        dev = (((z + sign + ZN) % ZN) * 2 + 1 - core, x, y)
        return remote(ref, ref, both_s.at[way], both_r.at[way], dev)

    def sibling(ch, d, receive=False):
        s = (z + d + ZN) % ZN
        ref = ug.at[ch, s * 2 + (1 - core if receive else core)]
        return remote(ref, ref, sib_s.at[ch, d % ZN], sib_r.at[ch, d % ZN], sib)

    def goes(way, step, half):
        return step < 3 or half == way

    def ring_own(ch):
        for way in range(2):
            ring(ch, way, 0, 0).start()

    def ring_step(ch, step):
        if step == 0:
            for sub in (1, 2, 3):
                a2a(ch, sub, True).wait_recv()
                for way in range(2):
                    ring(ch, way, 0, sub).start()
            sibling(ch, 0).start()
            return
        for half in range(2):
            for way in range(2):
                if step == 1:
                    ring(ch, way, 0, 2 * half, True).wait_recv()
                    ring(ch, way, 0, 2 * half + 1, True).wait_recv()
                elif goes(way, step - 1, half):
                    ring(ch, way, step - 1, half, True).wait_recv()
                if step < 4 and goes(way, step, half):
                    ring(ch, way, step, half).start()
                    if step == 3 and ch == CH - 1:
                        both(way).start()
        if step == 4:
            if ch < CH - 1:
                sibling(ch, step).start()
        else:
            sibling(ch, -step).start()
            sibling(ch, step).start()

    def wait_sibling(ch):
        for d in range(ZN):
            if d == 4 and ch == CH - 1:
                both(0, True).wait_recv()
                both(1, True).wait_recv()
            else:
                sibling(ch, d, True).wait_recv()

    def a_first(d, receive=False):
        ref = la.at[0, (x - d + 4) % 4 if receive else x, pl.ds(0, 2)]
        return remote(ref, ref, a1_s.at[d - 1], a1_r.at[d - 1], xdev(d))

    def a_next(e, sub, receive=False):
        xx = (x - e + 4) % 4
        dst = la.at[sub, xx, pl.ds(0, 2)]
        src = dst if receive else la.at[0, xx, pl.ds(0, 2)]
        return remote(src, dst, a2_s.at[e, sub - 1], a2_r.at[e, sub - 1], ydev(SUBS[sub]))

    def b_first(sub, receive=False):
        dst = lb.at[sub, x, pl.ds(0, 3)]
        src = dst if receive else lb.at[0, x, pl.ds(0, 3)]
        return remote(src, dst, b1_s.at[sub - 1], b1_r.at[sub - 1], ydev(SUBS[sub]))

    def b_next(sub, d, receive=False):
        ref = lb.at[sub, (x - d + 4) % 4 if receive else x, pl.ds(0, 3)]
        return remote(ref, ref, b2_s.at[sub, d - 1], b2_r.at[sub, d - 1], xdev(d))

    def ship(ch, d, receive=False):
        dst = out_ref.at[ch, (y - d + 4) % 4 if receive else y]
        src = dst if receive else snd.at[ch, (y + d) % 4]
        return remote(src, dst, shp_s.at[ch, d - 1], shp_r.at[ch, d - 1], ydev(d))

    def lower_prep():
        first = jnp.dot(
            lp_ref[0].reshape(128, B), piv_ref[0], preferred_element_type=jnp.float32
        ).astype(jnp.bfloat16)
        la[0, x, 0:2] = first.reshape(2, 64, B)
        for d in (1, 3, 2):
            a_first(d).start()
        link = jnp.dot(ll_ref[...], piv_ref[0], preferred_element_type=jnp.float32)
        lb[0, x, 2] = link.astype(jnp.bfloat16)
        wide = first.astype(jnp.float32)
        pieces = []
        for g in range(2):
            sg = low_ref[2 + g, y]
            hit0 = jnp.where((sg >= 0) & (sg == low_ref[0, y]), 1.0, 0.0)
            hit1 = jnp.where((sg >= 0) & (sg == low_ref[1, y]), 1.0, 0.0)
            pieces.append(wide[:64] * hit0 + wide[64:] * hit1)
        carried = jnp.concatenate(pieces, axis=0).astype(jnp.bfloat16)
        term = jnp.dot(carried, ul_ref[...], preferred_element_type=jnp.float32)
        diff = (lp_ref[1].reshape(128, B).astype(jnp.float32) - term).astype(jnp.bfloat16)
        second = jnp.dot(diff, piv_ref[1], preferred_element_type=jnp.float32).astype(jnp.bfloat16)
        lb[0, x, 0:2] = second.reshape(2, 64, B)
        for sub in (1, 2, 3):
            b_first(sub).start()
        for sub in (1, 2, 3):
            a_next(0, sub).start()
        for d in (1, 3, 2):
            b_next(0, d).start()

    def lower_forward():
        for i in range(3):
            sub, e = i + 1, (1, 3, 2)[i]
            b_first(sub, True).wait_recv()
            for d in (1, 3, 2):
                b_next(sub, d).start()
            a_first(e, True).wait_recv()
            for s in (1, 2, 3):
                a_next(e, s).start()

    def lower_select():
        for e in range(4):
            for s in (1, 2, 3):
                a_next(e, s, True).wait_recv()
        for s in range(4):
            for d in (1, 2, 3):
                b_next(s, d, True).wait_recv()
        for s in range(4):
            q = rep_of(s)
            for k, store in ((0, la), (1, lb)):
                s0 = low_ref[2 * k, q]
                s1 = low_ref[2 * k + 1, q]
                for a in range(2):
                    at = jnp.where(s0 == a, 0, jnp.where(s1 == a, 1, 2 + k))
                    for xx in range(4):
                        lsel[a, xx * 64 : xx * 64 + 64, (2 * s + k) * B : (2 * s + k + 1) * B] = (
                            store[s, xx, at]
                        )

    def turn(ch):
        def step(s, carry):
            for k in range(2):
                for g in range(GROUPS):
                    rows = pl.ds(pl.multiple_of(s * PIECE + (k * GROUPS + g) * 16, 16), 16)
                    block = ug[ch, :, rows, :].reshape(B, 128)
                    ut[s, k, GS * g : GS * g + GS] = block.T.reshape(GS, W, B)
            return carry

        lax.fori_loop(0, 4, step, 0)

    def arrange():
        def step(b, carry):
            rows = pl.ds(pl.multiple_of(b * W, W), W)
            for s in range(4):
                q = rep_of(s)
                lhs[rows, 2 * s * B : 2 * s * B + B] = ut[s, 0, tab_ref[b, q * 3]]
                lhs[rows, (2 * s + 1) * B : (2 * s + 2) * B] = ut[s, 1, tab_ref[b, q * 3 + 1]]
                acb[s, rows, :] = ut[s, 0, tab_ref[b, q * 3 + 2]]
            return carry

        lax.fori_loop(0, 32, step, 0)

    def second_upper():
        for s in range(4):
            link = lb[s, :, 2].reshape(B, B)
            shift = lax.dot_general(acb[s], link, NT, preferred_element_type=jnp.float32)
            cols = slice((2 * s + 1) * B, (2 * s + 2) * B)
            lhs[:, cols] = (lhs[:, cols].astype(jnp.float32) - shift).astype(jnp.bfloat16)

    def multiply():
        for a in range(2):
            prod = lax.dot_general(lhs[...], lsel[a], NT, preferred_element_type=jnp.float32)
            ctb[32 * a : 32 * a + 32] = prod.astype(jnp.bfloat16).reshape(32, W, B)

    def choose(ch):
        def step(i, carry):
            for j in range(16):
                snd[ch, i, j * W : j * W + W, :] = ctb[own_ref[0, i * 16 + j]]
            return carry

        lax.fori_loop(0, 4, step, 0)

    def local_out(ch):
        return pltpu.make_async_copy(snd.at[ch, y], out_ref.at[ch, y], loc_s.at[ch])

    def p1(ch):
        wait_sibling(ch)
        turn(ch)

    def p2():
        arrange()
        second_upper()

    def p4(ch):
        choose(ch)
        for d in (1, 3, 2):
            ship(ch, d).start()
        local_out(ch).start()

    def make_table():
        column = lax.broadcasted_iota(jnp.int32, (32, 128), 1)
        name = lax.broadcasted_iota(jnp.int32, (32, SLOTS), 0)
        at = lax.broadcasted_iota(jnp.int32, (32, SLOTS), 1)
        table = jnp.zeros((32, 128), jnp.int32)
        for q in range(4):
            found = [
                jnp.min(
                    jnp.where(slots_ref[q, k : k + 1, :] == name, at, SLOTS),
                    axis=1,
                    keepdims=True,
                )
                for k in range(2)
            ]
            found.append(jnp.where(found[1] < SLOTS, found[0], SLOTS))
            for k in range(3):
                table = jnp.where(column == 3 * q + k, found[k], table)
        tab_vmem[...] = table
        pltpu.make_async_copy(tab_vmem, tab_ref, in_s.at[6]).start()

    def zero_fill():
        for s in range(4):
            for k in range(2):
                ut[s, k, SLOTS] = jnp.zeros((W, B), jnp.bfloat16)
            for xx in range(4):
                la[s, xx, 2] = jnp.zeros((64, B), jnp.bfloat16)
                lb[s, xx, 3] = jnp.zeros((64, B), jnp.bfloat16)

    def a2a_start(ch):
        for sub in (1, 2, 3):
            a2a(ch, sub).start()

    loads[0].wait()
    pack(0)
    pl.semaphore_wait(bar, len(partners))
    a2a_start(0)
    ring_own(0)
    pack(1)
    a2a_start(1)
    ring_own(1)
    for ch in (2, 3):
        pack(ch)
        ring_own(ch)
    for load in loads[1:]:
        load.wait()
    lower_prep()
    for what, ch in EVENTS:
        if what == "a2a":
            a2a_start(ch)
        elif what == "forward":
            zero_fill()
            lower_forward()
            make_table()
        elif what == "select":
            lower_select()
            pltpu.make_async_copy(tab_vmem, tab_ref, in_s.at[6]).wait()
        elif what == "p1":
            p1(ch)
        elif what == "p2":
            p2()
        elif what == "p3":
            multiply()
        elif what == "p4":
            p4(ch)
        else:
            ring_step(ch, int(what))

    for ch in range(CH):
        for sub in (1, 2, 3):
            a2a(ch, sub).wait_send()
        for way in range(2):
            for step in range(4):
                for half in range(2 if step else 4):
                    if goes(way, step, half):
                        ring(ch, way, step, half).wait_send()
        for d in range(ZN):
            if d == 4 and ch == CH - 1:
                both(0).wait_send()
                both(1).wait_send()
            else:
                sibling(ch, d).wait_send()
    for i in range(4):
        for d in (1, 2, 3):
            a_next(i, d).wait_send()
            b_next(i, d).wait_send()
            if i == 0:
                a_first(d).wait_send()
                b_first(d).wait_send()
    for ch in range(CH):
        local_out(ch).wait()
        for d in (1, 2, 3):
            ship(ch, d).wait_send()
            ship(ch, d, True).wait_recv()


def finish_kernel(front_hbm, got_hbm, out_hbm, front, got, out, front_s, got_s, out_s):
    got_copies = [
        pltpu.make_async_copy(
            got_hbm.at[:, :, pl.ds(4 * W * i, 4 * W)],
            got.at[:, :, pl.ds(4 * W * i, 4 * W)],
            got_s.at[i],
        )
        for i in range(4)
    ]

    def fetch(i):
        return pltpu.make_async_copy(front_hbm.at[i], front.at[i], front_s.at[i])

    def store(i):
        return pltpu.make_async_copy(out.at[i], out_hbm.at[i], out_s.at[i])

    for i in range(16):
        if i % 4 == 0:
            got_copies[i // 4].start()
        fetch(i).start()
    for i in range(16):
        if i % 4 == 0:
            got_copies[i // 4].wait()
        fetch(i).wait()
        block = got[:, :, W * i : W * i + W].reshape(B, B)
        out[i] = front[i] - block.T.astype(jnp.float32)
        store(i).start()
    for i in range(16):
        store(i).wait()


def body(
    front,
    pivots,
    upper_link,
    lower_link,
    lower_panels,
    upper_panels,
    lower_slots,
    upper_slots,
    owner_map,
):
    smem = pl.BlockSpec(memory_space=pltpu.SMEM)
    hbm = pl.BlockSpec(memory_space=pl.ANY)
    dma = pltpu.SemaphoreType.DMA
    bf = jnp.bfloat16
    got = pl.pallas_call(
        main_kernel,
        out_shape=jax.ShapeDtypeStruct((CH, 4, 16 * W, B), bf),
        in_specs=[smem] * 2 + [hbm] * 6,
        out_specs=hbm,
        scratch_shapes=[
            pltpu.VMEM((4, 2, SLOTS), jnp.int32),
            pltpu.VMEM((32, 128), jnp.int32),
            pltpu.SMEM((32, 128), jnp.int32),
            pltpu.VMEM((2, GROUPS, GS, 16, B), bf),
            pltpu.VMEM((2, 2, 64, B), bf),
            pltpu.VMEM((2, B, B), bf),
            pltpu.VMEM((B, B), bf),
            pltpu.VMEM((64, B), bf),
            pltpu.VMEM((CH, 4, PIECE, 128), bf),
            pltpu.VMEM((CH, 16, 4 * PIECE, 128), bf),
            pltpu.VMEM((4, 2, SLOTS + 1, W, B), bf),
            pltpu.VMEM((4, 4, 3, 64, B), bf),
            pltpu.VMEM((4, 4, 4, 64, B), bf),
            pltpu.VMEM((2, B, 8 * B), bf),
            pltpu.VMEM((32 * W, 8 * B), bf),
            pltpu.VMEM((4, 32 * W, B), bf),
            pltpu.VMEM((64, W, B), bf),
            pltpu.VMEM((CH, 4, 16 * W, B), bf),
            dma((7,)),
            dma((CH, 3)),
            dma((CH, 3)),
            dma((CH, 2, 4, 4)),
            dma((CH, 2, 4, 4)),
            dma((CH, ZN)),
            dma((CH, ZN)),
            dma((2,)),
            dma((2,)),
            dma((3,)),
            dma((3,)),
            dma((4, 3)),
            dma((4, 3)),
            dma((3,)),
            dma((3,)),
            dma((4, 3)),
            dma((4, 3)),
            dma((CH, 3)),
            dma((CH, 3)),
            dma((CH,)),
        ],
        compiler_params=pltpu.CompilerParams(
            collective_id=0, has_side_effects=True, vmem_limit_bytes=60 << 20
        ),
    )(
        jnp.transpose(lower_slots, (1, 2, 0)).reshape(4, 4),
        owner_map,
        upper_slots,
        upper_panels[0].reshape(2, GROUPS, GS, 16, B),
        lower_panels[0],
        pivots[0],
        upper_link[0],
        lower_link[0],
    )
    return pl.pallas_call(
        finish_kernel,
        out_shape=jax.ShapeDtypeStruct(front.shape, front.dtype),
        in_specs=[hbm, hbm],
        out_specs=hbm,
        scratch_shapes=[
            pltpu.VMEM((16, B, B), jnp.float32),
            pltpu.VMEM((CH, 4, 16 * W, B), bf),
            pltpu.VMEM((16, B, B), jnp.float32),
            dma((16,)),
            dma((4,)),
            dma((16,)),
        ],
        compiler_params=pltpu.CompilerParams(vmem_limit_bytes=60 << 20),
    )(front, got)


def solution(mesh):
    return jax.shard_map(
        body,
        mesh=mesh,
        in_specs=(
            P(("row", "col", "rep"), None, None),
            P("rep", None, None, None),
            P("rep", None, None),
            P("rep", None, None),
            P("rep", None, "row", "col", None),
            P("rep", None, "col", "row", None),
            P(None, None, "row"),
            P(None, None, "col"),
            P(("row", "col"), None),
        ),
        out_specs=P(("row", "col", "rep"), None, None),
        check_vma=False,
    )
```

```python
import jax
import jax.numpy as jnp
from jax import lax
from jax.experimental import pallas as pl
from jax.experimental.pallas import tpu as pltpu
from jax.sharding import PartitionSpec as P

MESH = pl.DeviceIdType.MESH
NT = (((1,), (1,)), ((), ()))
B = 256
CH = 4
W = 16
SLOTS = 24
GS = 8
GROUPS = 3
PIECE = 2 * GROUPS * 16
SUBS = (0, 1, 3, 2)
ZN = 8
EVENTS = (
    ("0", 0),
    ("a2a", 2),
    ("0", 1),
    ("a2a", 3),
    ("1", 0),
    ("1", 1),
    ("forward", 0),
    ("2", 0),
    ("0", 2),
    ("2", 1),
    ("3", 0),
    ("1", 2),
    ("4", 0),
    ("0", 3),
    ("p1", 0),
    ("3", 1),
    ("2", 2),
    ("select", 0),
    ("p2", 0),
    ("4", 1),
    ("1", 3),
    ("p3", 0),
    ("p4", 0),
    ("3", 2),
    ("p1", 1),
    ("p2", 0),
    ("2", 3),
    ("p3", 0),
    ("p4", 1),
    ("4", 2),
    ("3", 3),
    ("p1", 2),
    ("p2", 0),
    ("4", 3),
    ("p3", 0),
    ("p4", 2),
    ("p1", 3),
    ("p2", 0),
    ("p3", 0),
    ("p4", 3),
)


def main_kernel(
    low_ref,
    own_ref,
    slots_hbm,
    u_hbm,
    lp_hbm,
    piv_hbm,
    ul_hbm,
    ll_hbm,
    out_ref,
    slots_ref,
    tab_vmem,
    tab_ref,
    u_ref,
    lp_ref,
    piv_ref,
    ul_ref,
    ll_ref,
    pk,
    ug,
    ut,
    la,
    lb,
    lsel,
    lhs,
    acb,
    ctb,
    snd,
    in_s,
    a2a_s,
    a2a_r,
    ring_s,
    ring_r,
    sib_r,
    a1_s,
    a1_r,
    a2_s,
    a2_r,
    b1_s,
    b1_r,
    b2_s,
    b2_r,
    shp_s,
    shp_r,
    loc_s,
):
    row = lax.axis_index("row")
    x = lax.axis_index("col")
    y = lax.axis_index("rep")
    z = row // 2
    core = row % 2

    def ydev(d):
        return (row, x, (y + d) % 4)

    def xdev(d):
        return (row, (x + d) % 4, y)

    def zdev(d):
        return (((z + d + ZN) % ZN) * 2 + core, x, y)

    sib = (z * 2 + 1 - core, x, y)

    def src_of(d):
        return ((z + d + ZN) % ZN) * 2 + core

    def rep_of(sub):
        return (y - SUBS[sub] + 4) % 4

    loads = [
        pltpu.make_async_copy(u_hbm, u_ref, in_s.at[0]),
        pltpu.make_async_copy(lp_hbm, lp_ref, in_s.at[1]),
        pltpu.make_async_copy(piv_hbm, piv_ref, in_s.at[2]),
        pltpu.make_async_copy(ul_hbm, ul_ref, in_s.at[3]),
        pltpu.make_async_copy(
            ll_hbm.at[pl.ds(pl.multiple_of(x * 64, 64), 64)], ll_ref, in_s.at[4]
        ),
    ]
    loads.append(pltpu.make_async_copy(slots_hbm, slots_ref, in_s.at[5]))
    for load in loads:
        load.start()
    bar = pltpu.get_barrier_semaphore()
    partners = [ydev(1), ydev(2), ydev(3), xdev(1), xdev(2), xdev(3), zdev(1), zdev(-1), sib]
    partners += [(((z + d + ZN) % ZN) * 2 + 1 - core, x, y) for d in (1, -1)]
    for p in partners:
        pl.semaphore_signal(bar, inc=1, device_id=p, device_id_type=MESH)

    def remote(src, dst, ss, rs, dev):
        return pltpu.make_async_remote_copy(
            src_ref=src, dst_ref=dst, send_sem=ss, recv_sem=rs, device_id=dev, device_id_type=MESH
        )

    def pack(ch):
        tile = 128 * (ch // 2)
        first = 64 * (ch % 2)
        parts = [
            u_ref[:, :, j, :, tile : tile + 128].reshape(2 * GROUPS * 16, 128) for j in range(GS)
        ]
        for yy in range(4):
            at = first + W * yy
            piece = jnp.concatenate([p[:, at : at + W] for p in parts], axis=1)
            pk[ch, yy] = piece
        ug[ch, row, 0:PIECE] = pk[ch, y]

    def a2a(ch, sub, receive=False):
        d = SUBS[sub]
        sems = (a2a_s.at[0], a2a_r.at[ch, sub - 1], ydev(d))
        ref = ug.at[ch, row, pl.ds(sub * PIECE, PIECE)]
        return remote(ref if receive else pk.at[ch, (y + d) % 4], ref, *sems)

    def ring(ch, way, step, part, receive=False):
        sign = 1 if way == 0 else -1
        origin = src_of(-sign * (step + 1 if receive else step))
        if step == 0 and not receive:
            ref = ug.at[ch, origin, pl.ds(part * PIECE, PIECE)]
            slot = part // 2
        else:
            ref = ug.at[ch, origin, pl.ds(2 * part * PIECE, 2 * PIECE)]
            slot = 2 * step + part if step < 3 else 6
        return remote(ref, ref, ring_s.at[ch], ring_r.at[ch, way, slot], zdev(sign))

    def both(way):
        sign = 1 if way == 0 else -1
        ref = ug.at[CH - 1, src_of(-3 * sign), pl.ds(2 * way * PIECE, 2 * PIECE)]
        dev = (((z + sign + ZN) % ZN) * 2 + 1 - core, x, y)
        return remote(ref, ref, ring_s.at[CH - 1], sib_r.at[CH - 1], dev)

    def sibling(ch, d):
        ref = ug.at[ch, src_of(d)]
        return remote(ref, ref, ring_s.at[ch], sib_r.at[ch], sib)

    def goes(way, step, half):
        return step < 3 or half == way

    def ring_own(ch):
        for way in range(2):
            ring(ch, way, 0, 0).start()

    def ring_step(ch, step):
        if step == 0:
            for sub in (1, 2, 3):
                a2a(ch, sub, True).wait_recv()
                for way in range(2):
                    ring(ch, way, 0, sub).start()
            sibling(ch, 0).start()
            return
        for half in range(2):
            for way in range(2):
                if goes(way, step - 1, half):
                    ring(ch, way, step - 1, half, True).wait_recv()
                if step < 4 and goes(way, step, half):
                    ring(ch, way, step, half).start()
                    if step == 3 and ch == CH - 1:
                        both(way).start()
        if step == 4:
            if ch < CH - 1:
                sibling(ch, step).start()
        else:
            sibling(ch, -step).start()
            sibling(ch, step).start()

    def wait_sibling(ch):
        ref = ug.at[ch, pl.ds(0, ZN)]
        remote(ref, ref, ring_s.at[ch], sib_r.at[ch], sib).wait_recv()

    def a_first(d, receive=False):
        ref = la.at[0, (x - d + 4) % 4 if receive else x, pl.ds(0, 2)]
        return remote(ref, ref, a1_s.at[0], a1_r.at[d - 1], xdev(d))

    def a_next(e, sub, receive=False):
        xx = (x - e + 4) % 4
        dst = la.at[sub, xx, pl.ds(0, 2)]
        src = dst if receive else la.at[0, xx, pl.ds(0, 2)]
        return remote(src, dst, a2_s.at[0], a2_r.at[0], ydev(SUBS[sub]))

    def b_first(sub, receive=False):
        dst = lb.at[sub, x, pl.ds(0, 3)]
        src = dst if receive else lb.at[0, x, pl.ds(0, 3)]
        return remote(src, dst, b1_s.at[0], b1_r.at[sub - 1], ydev(SUBS[sub]))

    def b_next(sub, d, receive=False):
        ref = lb.at[sub, (x - d + 4) % 4 if receive else x, pl.ds(0, 3)]
        return remote(ref, ref, b2_s.at[0], b2_r.at[0], xdev(d))

    def ship(ch, d, receive=False):
        dst = out_ref.at[ch, (y - d + 4) % 4 if receive else y]
        src = dst if receive else snd.at[ch, (y + d) % 4]
        return remote(src, dst, shp_s.at[0], shp_r.at[0], ydev(d))

    def lower_prep():
        first = jnp.dot(
            lp_ref[0].reshape(128, B), piv_ref[0], preferred_element_type=jnp.float32
        ).astype(jnp.bfloat16)
        la[0, x, 0:2] = first.reshape(2, 64, B)
        for d in (1, 3, 2):
            a_first(d).start()
        link = jnp.dot(ll_ref[...], piv_ref[0], preferred_element_type=jnp.float32)
        lb[0, x, 2] = link.astype(jnp.bfloat16)
        wide = first.astype(jnp.float32)
        pieces = []
        for g in range(2):
            sg = low_ref[2 + g, y]
            hit0 = jnp.where((sg >= 0) & (sg == low_ref[0, y]), 1.0, 0.0)
            hit1 = jnp.where((sg >= 0) & (sg == low_ref[1, y]), 1.0, 0.0)
            pieces.append(wide[:64] * hit0 + wide[64:] * hit1)
        carried = jnp.concatenate(pieces, axis=0).astype(jnp.bfloat16)
        term = jnp.dot(carried, ul_ref[...], preferred_element_type=jnp.float32)
        diff = (lp_ref[1].reshape(128, B).astype(jnp.float32) - term).astype(jnp.bfloat16)
        second = jnp.dot(diff, piv_ref[1], preferred_element_type=jnp.float32).astype(jnp.bfloat16)
        lb[0, x, 0:2] = second.reshape(2, 64, B)
        for sub in (1, 2, 3):
            b_first(sub).start()
        for sub in (1, 2, 3):
            a_next(0, sub).start()
        for d in (1, 3, 2):
            b_next(0, d).start()

    def lower_forward():
        for i in range(3):
            sub, e = i + 1, (1, 3, 2)[i]
            b_first(sub, True).wait_recv()
            for d in (1, 3, 2):
                b_next(sub, d).start()
            a_first(e, True).wait_recv()
            for s in (1, 2, 3):
                a_next(e, s).start()

    def lower_select():
        ref = la.at[pl.ds(1, 3), :, pl.ds(0, 2)]
        remote(ref, ref, a2_s.at[0], a2_r.at[0], ydev(1)).wait_recv()
        ref = lb.at[pl.ds(0, 3), :, pl.ds(0, 3)]
        remote(ref, ref, b2_s.at[0], b2_r.at[0], xdev(1)).wait_recv()
        for s in range(4):
            q = rep_of(s)
            for k, store in ((0, la), (1, lb)):
                s0 = low_ref[2 * k, q]
                s1 = low_ref[2 * k + 1, q]
                for a in range(2):
                    at = jnp.where(s0 == a, 0, jnp.where(s1 == a, 1, 2 + k))
                    for xx in range(4):
                        lsel[a, xx * 64 : xx * 64 + 64, (2 * s + k) * B : (2 * s + k + 1) * B] = (
                            store[s, xx, at]
                        )

    def turn(ch):
        def step(s, carry):
            for k in range(2):
                for g in range(GROUPS):
                    rows = pl.ds(pl.multiple_of(s * PIECE + (k * GROUPS + g) * 16, 16), 16)
                    block = ug[ch, :, rows, :].reshape(B, 128)
                    ut[s, k, GS * g : GS * g + GS] = block.T.reshape(GS, W, B)
            return carry

        lax.fori_loop(0, 4, step, 0)

    def arrange():
        def step(b, carry):
            rows = pl.ds(pl.multiple_of(b * W, W), W)
            for s in range(4):
                q = rep_of(s)
                lhs[rows, 2 * s * B : 2 * s * B + B] = ut[s, 0, tab_ref[b, q * 3]]
                lhs[rows, (2 * s + 1) * B : (2 * s + 2) * B] = ut[s, 1, tab_ref[b, q * 3 + 1]]
                acb[s, rows, :] = ut[s, 0, tab_ref[b, q * 3 + 2]]
            return carry

        lax.fori_loop(0, 32, step, 0)

    def second_upper():
        for s in range(4):
            link = lb[s, :, 2].reshape(B, B)
            shift = lax.dot_general(acb[s], link, NT, preferred_element_type=jnp.float32)
            cols = slice((2 * s + 1) * B, (2 * s + 2) * B)
            lhs[:, cols] = (lhs[:, cols].astype(jnp.float32) - shift).astype(jnp.bfloat16)

    def multiply():
        for a in range(2):
            prod = lax.dot_general(lhs[...], lsel[a], NT, preferred_element_type=jnp.float32)
            ctb[32 * a : 32 * a + 32] = prod.astype(jnp.bfloat16).reshape(32, W, B)

    def choose(ch):
        def step(i, carry):
            for j in range(16):
                snd[ch, i, j * W : j * W + W, :] = ctb[own_ref[0, i * 16 + j]]
            return carry

        lax.fori_loop(0, 4, step, 0)

    def local_out(ch):
        return pltpu.make_async_copy(snd.at[ch, y], out_ref.at[ch, y], loc_s.at[0])

    def p1(ch):
        wait_sibling(ch)
        turn(ch)

    def p2():
        arrange()
        second_upper()

    def p4(ch):
        choose(ch)
        for d in (1, 3, 2):
            ship(ch, d).start()
        local_out(ch).start()

    def make_table():
        column = lax.broadcasted_iota(jnp.int32, (32, 128), 1)
        name = lax.broadcasted_iota(jnp.int32, (32, SLOTS), 0)
        at = lax.broadcasted_iota(jnp.int32, (32, SLOTS), 1)
        table = jnp.zeros((32, 128), jnp.int32)
        for q in range(4):
            found = [
                jnp.min(
                    jnp.where(slots_ref[q, k : k + 1, :] == name, at, SLOTS),
                    axis=1,
                    keepdims=True,
                )
                for k in range(2)
            ]
            found.append(jnp.where(found[1] < SLOTS, found[0], SLOTS))
            for k in range(3):
                table = jnp.where(column == 3 * q + k, found[k], table)
        tab_vmem[...] = table
        pltpu.make_async_copy(tab_vmem, tab_ref, in_s.at[6]).start()

    def zero_fill():
        for s in range(4):
            for k in range(2):
                ut[s, k, SLOTS] = jnp.zeros((W, B), jnp.bfloat16)
            for xx in range(4):
                la[s, xx, 2] = jnp.zeros((64, B), jnp.bfloat16)
                lb[s, xx, 3] = jnp.zeros((64, B), jnp.bfloat16)

    def a2a_start(ch):
        for sub in (1, 2, 3):
            a2a(ch, sub).start()

    loads[0].wait()
    pack(0)
    pl.semaphore_wait(bar, len(partners))
    a2a_start(0)
    ring_own(0)
    pack(1)
    a2a_start(1)
    ring_own(1)
    for ch in (2, 3):
        pack(ch)
        ring_own(ch)
    for load in loads[1:]:
        load.wait()
    lower_prep()
    for what, ch in EVENTS:
        if what == "a2a":
            a2a_start(ch)
        elif what == "forward":
            zero_fill()
            lower_forward()
            make_table()
        elif what == "select":
            lower_select()
            pltpu.make_async_copy(tab_vmem, tab_ref, in_s.at[6]).wait()
        elif what == "p1":
            p1(ch)
        elif what == "p2":
            p2()
        elif what == "p3":
            multiply()
        elif what == "p4":
            p4(ch)
        else:
            ring_step(ch, int(what))

    def sent(ref, sem):
        remote(ref, ref, sem, shp_r.at[0], sib).wait_send()

    sent(ug.at[0, pl.ds(0, 3)], a2a_s.at[0])
    for ch in range(CH):
        sent(ug.at[ch, pl.ds(0, 15)], ring_s.at[ch])
    sent(la.at[0, pl.ds(0, 3), pl.ds(0, 2)], a1_s.at[0])
    sent(la.at[pl.ds(1, 3), :, pl.ds(0, 2)], a2_s.at[0])
    sent(lb.at[0, pl.ds(0, 3), pl.ds(0, 3)], b1_s.at[0])
    sent(lb.at[pl.ds(0, 3), :, pl.ds(0, 3)], b2_s.at[0])
    sent(snd.at[pl.ds(0, 3)], shp_s.at[0])
    pltpu.make_async_copy(snd.at[0], out_ref.at[0], loc_s.at[0]).wait()
    ref = out_ref.at[pl.ds(0, 3)]
    remote(ref, ref, shp_s.at[0], shp_r.at[0], ydev(1)).wait_recv()


def finish_kernel(front_hbm, got_hbm, out_hbm, front, got, out, front_s, got_s, out_s):
    got_copies = [
        pltpu.make_async_copy(
            got_hbm.at[:, :, pl.ds(4 * W * i, 4 * W)],
            got.at[:, :, pl.ds(4 * W * i, 4 * W)],
            got_s.at[i],
        )
        for i in range(4)
    ]

    def fetch(i):
        return pltpu.make_async_copy(front_hbm.at[i], front.at[i], front_s.at[i])

    def store(i):
        return pltpu.make_async_copy(out.at[i], out_hbm.at[i], out_s.at[i])

    for i in range(16):
        if i % 4 == 0:
            got_copies[i // 4].start()
        fetch(i).start()
    for i in range(16):
        if i % 4 == 0:
            got_copies[i // 4].wait()
        fetch(i).wait()
        block = got[:, :, W * i : W * i + W].reshape(B, B)
        out[i] = front[i] - block.T.astype(jnp.float32)
        store(i).start()
    for i in range(16):
        store(i).wait()


def body(
    front,
    pivots,
    upper_link,
    lower_link,
    lower_panels,
    upper_panels,
    lower_slots,
    upper_slots,
    owner_map,
):
    smem = pl.BlockSpec(memory_space=pltpu.SMEM)
    hbm = pl.BlockSpec(memory_space=pl.ANY)
    dma = pltpu.SemaphoreType.DMA
    bf = jnp.bfloat16
    got = pl.pallas_call(
        main_kernel,
        out_shape=jax.ShapeDtypeStruct((CH, 4, 16 * W, B), bf),
        in_specs=[smem] * 2 + [hbm] * 6,
        out_specs=hbm,
        scratch_shapes=[
            pltpu.VMEM((4, 2, SLOTS), jnp.int32),
            pltpu.VMEM((32, 128), jnp.int32),
            pltpu.SMEM((32, 128), jnp.int32),
            pltpu.VMEM((2, GROUPS, GS, 16, B), bf),
            pltpu.VMEM((2, 2, 64, B), bf),
            pltpu.VMEM((2, B, B), bf),
            pltpu.VMEM((B, B), bf),
            pltpu.VMEM((64, B), bf),
            pltpu.VMEM((CH, 4, PIECE, 128), bf),
            pltpu.VMEM((CH, 16, 4 * PIECE, 128), bf),
            pltpu.VMEM((4, 2, SLOTS + 1, W, B), bf),
            pltpu.VMEM((4, 4, 3, 64, B), bf),
            pltpu.VMEM((4, 4, 4, 64, B), bf),
            pltpu.VMEM((2, B, 8 * B), bf),
            pltpu.VMEM((32 * W, 8 * B), bf),
            pltpu.VMEM((4, 32 * W, B), bf),
            pltpu.VMEM((64, W, B), bf),
            pltpu.VMEM((CH, 4, 16 * W, B), bf),
            dma((7,)),
            dma((1,)),
            dma((CH, 3)),
            dma((CH,)),
            dma((CH, 2, 7)),
            dma((CH,)),
            dma((1,)),
            dma((3,)),
            dma((1,)),
            dma((1,)),
            dma((1,)),
            dma((3,)),
            dma((1,)),
            dma((1,)),
            dma((1,)),
            dma((1,)),
            dma((1,)),
        ],
        compiler_params=pltpu.CompilerParams(
            collective_id=0, has_side_effects=True, vmem_limit_bytes=60 << 20
        ),
    )(
        jnp.transpose(lower_slots, (1, 2, 0)).reshape(4, 4),
        owner_map,
        upper_slots,
        upper_panels[0].reshape(2, GROUPS, GS, 16, B),
        lower_panels[0],
        pivots[0],
        upper_link[0],
        lower_link[0],
    )
    return pl.pallas_call(
        finish_kernel,
        out_shape=jax.ShapeDtypeStruct(front.shape, front.dtype),
        in_specs=[hbm, hbm],
        out_specs=hbm,
        scratch_shapes=[
            pltpu.VMEM((16, B, B), jnp.float32),
            pltpu.VMEM((CH, 4, 16 * W, B), bf),
            pltpu.VMEM((16, B, B), jnp.float32),
            dma((16,)),
            dma((4,)),
            dma((16,)),
        ],
        compiler_params=pltpu.CompilerParams(vmem_limit_bytes=60 << 20),
    )(front, got)


def solution(mesh):
    return jax.shard_map(
        body,
        mesh=mesh,
        in_specs=(
            P(("row", "col", "rep"), None, None),
            P("rep", None, None, None),
            P("rep", None, None),
            P("rep", None, None),
            P("rep", None, "row", "col", None),
            P("rep", None, "col", "row", None),
            P(None, None, "row"),
            P(None, None, "col"),
            P(("row", "col"), None),
        ),
        out_specs=P(("row", "col", "rep"), None, None),
        check_vma=False,
    )
```

```python
import jax
import jax.numpy as jnp
from jax import lax
from jax.experimental import pallas as pl
from jax.experimental.pallas import tpu as pltpu
from jax.sharding import PartitionSpec as P

MESH = pl.DeviceIdType.MESH
NT = (((1,), (1,)), ((), ()))
B = 256
CH = 4
W = 16
SLOTS = 24
GS = 8
GROUPS = 3
PIECE = 2 * GROUPS * 16
SUBS = (0, 1, 3, 2)
ZN = 8
EVENTS = (
    ("0", 0),
    ("a2a", 2),
    ("0", 1),
    ("a2a", 3),
    ("1", 0),
    ("1", 1),
    ("forward", 0),
    ("2", 0),
    ("0", 2),
    ("3", 0),
    ("2", 1),
    ("4", 0),
    ("1", 2),
    ("p1", 0),
    ("3", 1),
    ("0", 3),
    ("select", 0),
    ("p2", 0),
    ("4", 1),
    ("2", 2),
    ("p3", 0),
    ("p4", 0),
    ("1", 3),
    ("p1", 1),
    ("3", 2),
    ("p2", 0),
    ("2", 3),
    ("p3", 0),
    ("p4", 1),
    ("4", 2),
    ("3", 3),
    ("p1", 2),
    ("p2", 0),
    ("p3", 0),
    ("p4", 2),
    ("4", 3),
    ("p1", 3),
    ("p2", 0),
    ("p3", 0),
    ("p4", 3),
)


def main_kernel(
    low_ref,
    own_ref,
    slots_hbm,
    u_hbm,
    lp_hbm,
    piv_hbm,
    ul_hbm,
    ll_hbm,
    out_ref,
    slots_ref,
    tab_vmem,
    tab_ref,
    u_ref,
    lp_ref,
    piv_ref,
    ul_ref,
    ll_ref,
    pk,
    ug,
    ut,
    la,
    lb,
    lsel,
    lhs,
    acb,
    ctb,
    snd,
    in_s,
    a2a_s,
    a2a_r,
    ring_s,
    ring_r,
    sib_r,
    a1_s,
    a1_r,
    a2_s,
    a2_r,
    b1_s,
    b1_r,
    b2_s,
    b2_r,
    shp_s,
    shp_r,
    loc_s,
):
    row = lax.axis_index("row")
    x = lax.axis_index("col")
    y = lax.axis_index("rep")
    z = row // 2
    core = row % 2

    def ydev(d):
        return (row, x, (y + d) % 4)

    def xdev(d):
        return (row, (x + d) % 4, y)

    def zdev(d):
        return (((z + d + ZN) % ZN) * 2 + core, x, y)

    sib = (z * 2 + 1 - core, x, y)

    def src_of(d):
        return ((z + d + ZN) % ZN) * 2 + core

    def rep_of(sub):
        return (y - SUBS[sub] + 4) % 4

    loads = [
        pltpu.make_async_copy(u_hbm, u_ref, in_s.at[0]),
        pltpu.make_async_copy(lp_hbm, lp_ref, in_s.at[1]),
        pltpu.make_async_copy(piv_hbm, piv_ref, in_s.at[2]),
        pltpu.make_async_copy(ul_hbm, ul_ref, in_s.at[3]),
        pltpu.make_async_copy(
            ll_hbm.at[pl.ds(pl.multiple_of(x * 64, 64), 64)], ll_ref, in_s.at[4]
        ),
    ]
    loads.append(pltpu.make_async_copy(slots_hbm, slots_ref, in_s.at[5]))
    for load in loads:
        load.start()
    bar = pltpu.get_barrier_semaphore()
    partners = [ydev(1), ydev(2), ydev(3), xdev(1), xdev(2), xdev(3), zdev(1), zdev(-1), sib]
    partners += [(((z + d + ZN) % ZN) * 2 + 1 - core, x, y) for d in (1, -1)]
    for p in partners:
        pl.semaphore_signal(bar, inc=1, device_id=p, device_id_type=MESH)

    def remote(src, dst, ss, rs, dev):
        return pltpu.make_async_remote_copy(
            src_ref=src, dst_ref=dst, send_sem=ss, recv_sem=rs, device_id=dev, device_id_type=MESH
        )

    def pack(ch):
        tile = 128 * (ch // 2)
        first = 64 * (ch % 2)
        parts = [
            u_ref[:, :, j, :, tile : tile + 128].reshape(2 * GROUPS * 16, 128) for j in range(GS)
        ]
        for yy in range(4):
            at = first + W * yy
            piece = jnp.concatenate([p[:, at : at + W] for p in parts], axis=1)
            pk[ch, yy] = piece
        ug[ch, row, 0:PIECE] = pk[ch, y]

    def a2a(ch, sub, receive=False):
        d = SUBS[sub]
        sems = (a2a_s.at[0], a2a_r.at[ch], ydev(d))
        if receive:
            ref = ug.at[ch, row, pl.ds(PIECE, 3 * PIECE)]
            return remote(ref, ref, *sems)
        return remote(pk.at[ch, (y + d) % 4], ug.at[ch, row, pl.ds(sub * PIECE, PIECE)], *sems)

    def ring(ch, way, step, part, receive=False):
        sign = 1 if way == 0 else -1
        origin = src_of(-sign * (step + 1 if receive else step))
        fine = ch == CH - 1
        if fine or (step == 0 and not receive):
            ref = ug.at[ch, origin, pl.ds(part * PIECE, PIECE)]
        else:
            ref = ug.at[ch, origin, pl.ds(2 * part * PIECE, 2 * PIECE)]
        if fine:
            slot = 4 * step + part if step < 3 else 12 + part % 2
        elif step == 0 and not receive:
            slot = part // 2
        else:
            slot = 2 * step + part if step < 3 else 6
        sem = ring_r.at[ch + slot // 7, way, slot % 7]
        return remote(ref, ref, ring_s.at[0], sem, zdev(sign))

    def both(way, part):
        sign = 1 if way == 0 else -1
        ref = ug.at[CH - 1, src_of(-3 * sign), pl.ds(part * PIECE, PIECE)]
        dev = (((z + sign + ZN) % ZN) * 2 + 1 - core, x, y)
        return remote(ref, ref, ring_s.at[0], sib_r.at[CH - 1], dev)

    def sibling(ch, d):
        ref = ug.at[ch, src_of(d)]
        return remote(ref, ref, ring_s.at[0], sib_r.at[ch], sib)

    def goes(way, step, half):
        return step < 3 or half == way

    def ring_own(ch):
        for way in range(2):
            ring(ch, way, 0, 0).start()

    def ring_step(ch, step):
        if step == 0:
            a2a(ch, 1, True).wait_recv()
            for sub in (1, 2, 3):
                for way in range(2):
                    ring(ch, way, 0, sub).start()
            sibling(ch, 0).start()
            return
        fine = ch == CH - 1
        for part in range(4 if fine else 2):
            half = part // 2 if fine else part
            for way in range(2):
                if goes(way, step - 1, half):
                    ring(ch, way, step - 1, part, True).wait_recv()
                if step < 4 and goes(way, step, half):
                    ring(ch, way, step, part).start()
                    if step == 3 and fine:
                        both(way, part).start()
        if step == 4:
            if ch < CH - 1:
                sibling(ch, step).start()
        else:
            sibling(ch, -step).start()
            sibling(ch, step).start()

    def wait_sibling(ch):
        ref = ug.at[ch, pl.ds(0, ZN)]
        remote(ref, ref, ring_s.at[0], sib_r.at[ch], sib).wait_recv()

    def a_first(d, receive=False):
        ref = la.at[0, (x - d + 4) % 4 if receive else x, pl.ds(0, 2)]
        return remote(ref, ref, a1_s.at[0], a1_r.at[d - 1], xdev(d))

    def a_next(e, sub, receive=False):
        xx = (x - e + 4) % 4
        dst = la.at[sub, xx, pl.ds(0, 2)]
        src = dst if receive else la.at[0, xx, pl.ds(0, 2)]
        return remote(src, dst, a2_s.at[0], a2_r.at[0], ydev(SUBS[sub]))

    def b_first(sub, receive=False):
        dst = lb.at[sub, x, pl.ds(0, 3)]
        src = dst if receive else lb.at[0, x, pl.ds(0, 3)]
        return remote(src, dst, b1_s.at[0], b1_r.at[sub - 1], ydev(SUBS[sub]))

    def b_next(sub, d, receive=False):
        ref = lb.at[sub, (x - d + 4) % 4 if receive else x, pl.ds(0, 3)]
        return remote(ref, ref, b2_s.at[0], b2_r.at[0], xdev(d))

    def ship(ch, d, receive=False):
        dst = out_ref.at[ch, (y - d + 4) % 4 if receive else y]
        src = dst if receive else snd.at[ch, (y + d) % 4]
        return remote(src, dst, shp_s.at[0], shp_r.at[0], ydev(d))

    def lower_prep():
        first = jnp.dot(
            lp_ref[0].reshape(128, B), piv_ref[0], preferred_element_type=jnp.float32
        ).astype(jnp.bfloat16)
        la[0, x, 0:2] = first.reshape(2, 64, B)
        for d in (1, 3, 2):
            a_first(d).start()
        link = jnp.dot(ll_ref[...], piv_ref[0], preferred_element_type=jnp.float32)
        lb[0, x, 2] = link.astype(jnp.bfloat16)
        wide = first.astype(jnp.float32)
        pieces = []
        for g in range(2):
            sg = low_ref[2 + g, y]
            hit0 = jnp.where((sg >= 0) & (sg == low_ref[0, y]), 1.0, 0.0)
            hit1 = jnp.where((sg >= 0) & (sg == low_ref[1, y]), 1.0, 0.0)
            pieces.append(wide[:64] * hit0 + wide[64:] * hit1)
        carried = jnp.concatenate(pieces, axis=0).astype(jnp.bfloat16)
        term = jnp.dot(carried, ul_ref[...], preferred_element_type=jnp.float32)
        diff = (lp_ref[1].reshape(128, B).astype(jnp.float32) - term).astype(jnp.bfloat16)
        second = jnp.dot(diff, piv_ref[1], preferred_element_type=jnp.float32).astype(jnp.bfloat16)
        lb[0, x, 0:2] = second.reshape(2, 64, B)
        for sub in (1, 2, 3):
            b_first(sub).start()
        for sub in (1, 2, 3):
            a_next(0, sub).start()
        for d in (1, 3, 2):
            b_next(0, d).start()

    def lower_forward():
        for i in range(3):
            sub, e = i + 1, (1, 3, 2)[i]
            b_first(sub, True).wait_recv()
            for d in (1, 3, 2):
                b_next(sub, d).start()
            a_first(e, True).wait_recv()
            for s in (1, 2, 3):
                a_next(e, s).start()

    def lower_select():
        ref = la.at[pl.ds(1, 3), :, pl.ds(0, 2)]
        remote(ref, ref, a2_s.at[0], a2_r.at[0], ydev(1)).wait_recv()
        ref = lb.at[pl.ds(0, 3), :, pl.ds(0, 3)]
        remote(ref, ref, b2_s.at[0], b2_r.at[0], xdev(1)).wait_recv()
        for s in range(4):
            q = rep_of(s)
            for k, store in ((0, la), (1, lb)):
                s0 = low_ref[2 * k, q]
                s1 = low_ref[2 * k + 1, q]
                for a in range(2):
                    at = jnp.where(s0 == a, 0, jnp.where(s1 == a, 1, 2 + k))
                    for xx in range(4):
                        lsel[a, xx * 64 : xx * 64 + 64, (2 * s + k) * B : (2 * s + k + 1) * B] = (
                            store[s, xx, at]
                        )

    def turn(ch):
        def step(s, carry):
            for k in range(2):
                for g in range(GROUPS):
                    rows = pl.ds(pl.multiple_of(s * PIECE + (k * GROUPS + g) * 16, 16), 16)
                    block = ug[ch, :, rows, :].reshape(B, 128)
                    ut[s, k, GS * g : GS * g + GS] = block.T.reshape(GS, W, B)
            return carry

        lax.fori_loop(0, 4, step, 0)

    def arrange():
        def step(b, carry):
            rows = pl.ds(pl.multiple_of(b * W, W), W)
            for s in range(4):
                q = rep_of(s)
                lhs[rows, 2 * s * B : 2 * s * B + B] = ut[s, 0, tab_ref[b, q * 3]]
                lhs[rows, (2 * s + 1) * B : (2 * s + 2) * B] = ut[s, 1, tab_ref[b, q * 3 + 1]]
                acb[s, rows, :] = ut[s, 0, tab_ref[b, q * 3 + 2]]
            return carry

        lax.fori_loop(0, 32, step, 0)

    def second_upper():
        for s in range(4):
            link = lb[s, :, 2].reshape(B, B)
            shift = lax.dot_general(acb[s], link, NT, preferred_element_type=jnp.float32)
            cols = slice((2 * s + 1) * B, (2 * s + 2) * B)
            lhs[:, cols] = (lhs[:, cols].astype(jnp.float32) - shift).astype(jnp.bfloat16)

    def multiply():
        for a in range(2):
            prod = lax.dot_general(lhs[...], lsel[a], NT, preferred_element_type=jnp.float32)
            ctb[32 * a : 32 * a + 32] = prod.astype(jnp.bfloat16).reshape(32, W, B)

    def choose(ch):
        def step(i, carry):
            for j in range(16):
                snd[ch, i, j * W : j * W + W, :] = ctb[own_ref[0, i * 16 + j]]
            return carry

        lax.fori_loop(0, 4, step, 0)

    def local_out(ch):
        return pltpu.make_async_copy(snd.at[ch, y], out_ref.at[ch, y], loc_s.at[0])

    def p1(ch):
        wait_sibling(ch)
        turn(ch)

    def p2():
        arrange()
        second_upper()

    def p4(ch):
        choose(ch)
        for d in (1, 3, 2):
            ship(ch, d).start()
        local_out(ch).start()

    def make_table():
        column = lax.broadcasted_iota(jnp.int32, (32, 128), 1)
        name = lax.broadcasted_iota(jnp.int32, (32, SLOTS), 0)
        at = lax.broadcasted_iota(jnp.int32, (32, SLOTS), 1)
        table = jnp.zeros((32, 128), jnp.int32)
        for q in range(4):
            found = [
                jnp.min(
                    jnp.where(slots_ref[q, k : k + 1, :] == name, at, SLOTS),
                    axis=1,
                    keepdims=True,
                )
                for k in range(2)
            ]
            found.append(jnp.where(found[1] < SLOTS, found[0], SLOTS))
            for k in range(3):
                table = jnp.where(column == 3 * q + k, found[k], table)
        tab_vmem[...] = table
        pltpu.make_async_copy(tab_vmem, tab_ref, in_s.at[6]).start()

    def zero_fill():
        for s in range(4):
            for k in range(2):
                ut[s, k, SLOTS] = jnp.zeros((W, B), jnp.bfloat16)
            for xx in range(4):
                la[s, xx, 2] = jnp.zeros((64, B), jnp.bfloat16)
                lb[s, xx, 3] = jnp.zeros((64, B), jnp.bfloat16)

    def a2a_start(ch):
        for sub in (1, 2, 3):
            a2a(ch, sub).start()

    loads[0].wait()
    pack(0)
    pl.semaphore_wait(bar, len(partners))
    a2a_start(0)
    ring_own(0)
    pack(1)
    a2a_start(1)
    ring_own(1)
    for ch in (2, 3):
        pack(ch)
        ring_own(ch)
    for load in loads[1:]:
        load.wait()
    lower_prep()
    for what, ch in EVENTS:
        if what == "a2a":
            a2a_start(ch)
        elif what == "forward":
            zero_fill()
            lower_forward()
            make_table()
        elif what == "select":
            lower_select()
            pltpu.make_async_copy(tab_vmem, tab_ref, in_s.at[6]).wait()
        elif what == "p1":
            p1(ch)
        elif what == "p2":
            p2()
        elif what == "p3":
            multiply()
        elif what == "p4":
            p4(ch)
        else:
            ring_step(ch, int(what))

    def sent(ref, sem):
        remote(ref, ref, sem, shp_r.at[0], sib).wait_send()

    sent(ug.at[0, pl.ds(0, 3)], a2a_s.at[0])
    sent(ug.at[:, pl.ds(0, 15)], ring_s.at[0])
    sent(la.at[0, pl.ds(0, 3), pl.ds(0, 2)], a1_s.at[0])
    sent(la.at[pl.ds(1, 3), :, pl.ds(0, 2)], a2_s.at[0])
    sent(lb.at[0, pl.ds(0, 3), pl.ds(0, 3)], b1_s.at[0])
    sent(lb.at[pl.ds(0, 3), :, pl.ds(0, 3)], b2_s.at[0])
    sent(snd.at[pl.ds(0, 3)], shp_s.at[0])
    pltpu.make_async_copy(snd.at[0], out_ref.at[0], loc_s.at[0]).wait()
    ref = out_ref.at[pl.ds(0, 3)]
    remote(ref, ref, shp_s.at[0], shp_r.at[0], ydev(1)).wait_recv()


def finish_kernel(front_hbm, got_hbm, out_hbm, front, got, out, front_s, got_s, out_s):
    got_copies = [
        pltpu.make_async_copy(
            got_hbm.at[:, :, pl.ds(4 * W * i, 4 * W)],
            got.at[:, :, pl.ds(4 * W * i, 4 * W)],
            got_s.at[i],
        )
        for i in range(4)
    ]

    def fetch(i):
        return pltpu.make_async_copy(front_hbm.at[i], front.at[i], front_s.at[i])

    def store(i):
        return pltpu.make_async_copy(out.at[i], out_hbm.at[i], out_s.at[0])

    for i in range(16):
        if i % 4 == 0:
            got_copies[i // 4].start()
        fetch(i).start()
    for i in range(16):
        if i % 4 == 0:
            got_copies[i // 4].wait()
        fetch(i).wait()
        block = got[:, :, W * i : W * i + W].reshape(B, B)
        out[i] = front[i] - block.T.astype(jnp.float32)
        store(i).start()
    pltpu.make_async_copy(out, out_hbm, out_s.at[0]).wait()


def body(
    front,
    pivots,
    upper_link,
    lower_link,
    lower_panels,
    upper_panels,
    lower_slots,
    upper_slots,
    owner_map,
):
    smem = pl.BlockSpec(memory_space=pltpu.SMEM)
    hbm = pl.BlockSpec(memory_space=pl.ANY)
    dma = pltpu.SemaphoreType.DMA
    bf = jnp.bfloat16
    got = pl.pallas_call(
        main_kernel,
        out_shape=jax.ShapeDtypeStruct((CH, 4, 16 * W, B), bf),
        in_specs=[smem] * 2 + [hbm] * 6,
        out_specs=hbm,
        scratch_shapes=[
            pltpu.VMEM((4, 2, SLOTS), jnp.int32),
            pltpu.VMEM((32, 128), jnp.int32),
            pltpu.SMEM((32, 128), jnp.int32),
            pltpu.VMEM((2, GROUPS, GS, 16, B), bf),
            pltpu.VMEM((2, 2, 64, B), bf),
            pltpu.VMEM((2, B, B), bf),
            pltpu.VMEM((B, B), bf),
            pltpu.VMEM((64, B), bf),
            pltpu.VMEM((CH, 4, PIECE, 128), bf),
            pltpu.VMEM((CH, 16, 4 * PIECE, 128), bf),
            pltpu.VMEM((4, 2, SLOTS + 1, W, B), bf),
            pltpu.VMEM((4, 4, 3, 64, B), bf),
            pltpu.VMEM((4, 4, 4, 64, B), bf),
            pltpu.VMEM((2, B, 8 * B), bf),
            pltpu.VMEM((32 * W, 8 * B), bf),
            pltpu.VMEM((4, 32 * W, B), bf),
            pltpu.VMEM((64, W, B), bf),
            pltpu.VMEM((CH, 4, 16 * W, B), bf),
            dma((7,)),
            dma((1,)),
            dma((CH,)),
            dma((1,)),
            dma((CH + 1, 2, 7)),
            dma((CH,)),
            dma((1,)),
            dma((3,)),
            dma((1,)),
            dma((1,)),
            dma((1,)),
            dma((3,)),
            dma((1,)),
            dma((1,)),
            dma((1,)),
            dma((1,)),
            dma((1,)),
        ],
        compiler_params=pltpu.CompilerParams(
            collective_id=0, has_side_effects=True, vmem_limit_bytes=60 << 20
        ),
    )(
        jnp.transpose(lower_slots, (1, 2, 0)).reshape(4, 4),
        owner_map,
        upper_slots,
        upper_panels[0].reshape(2, GROUPS, GS, 16, B),
        lower_panels[0],
        pivots[0],
        upper_link[0],
        lower_link[0],
    )
    return pl.pallas_call(
        finish_kernel,
        out_shape=jax.ShapeDtypeStruct(front.shape, front.dtype),
        in_specs=[hbm, hbm],
        out_specs=hbm,
        scratch_shapes=[
            pltpu.VMEM((16, B, B), jnp.float32),
            pltpu.VMEM((CH, 4, 16 * W, B), bf),
            pltpu.VMEM((16, B, B), jnp.float32),
            dma((16,)),
            dma((4,)),
            dma((1,)),
        ],
        compiler_params=pltpu.CompilerParams(vmem_limit_bytes=60 << 20),
    )(front, got)


def solution(mesh):
    return jax.shard_map(
        body,
        mesh=mesh,
        in_specs=(
            P(("row", "col", "rep"), None, None),
            P("rep", None, None, None),
            P("rep", None, None),
            P("rep", None, None),
            P("rep", None, "row", "col", None),
            P("rep", None, "col", "row", None),
            P(None, None, "row"),
            P(None, None, "col"),
            P(("row", "col"), None),
        ),
        out_specs=P(("row", "col", "rep"), None, None),
        check_vma=False,
    )
```
